128 devices in a mesh: replica: 8 (over y_lo, z), fsdp: 16 (over y_hi, x, core).
Axes of the slice: x: 4, y: 4 (y_hi: 2, y_lo: 2; y = y_hi * 2 + y_lo), z: 4, core: 2. Of those that a mesh axis runs over, the one named last changes fastest.
Arguments:
- activations: bfloat16 [8, 4096, 4608], P('replica', 'fsdp'), may hold values from -6 to 6
- cotangent: bfloat16 [8, 4096, 2, 1024], P('replica', 'fsdp'), may hold values from -0.1796875 to 0.1796875
- weights: float32 [8, 4608, 2, 1024], P('replica', 'fsdp'), may hold values from -0.6 to 0.6
- first_moment: float32 [8, 4608, 2, 1024], P('replica', 'fsdp'), may hold values from -3 to 3
- second_moment: float32 [8, 4608, 2, 1024], P('replica', 'fsdp'), may hold values from 0.1 to 3
- anchor: float32 [4608, 1024], P('fsdp'), may hold values from -0.6 to 0.6
- momentum: float32 [4608, 1024], P('fsdp'), may hold values from -0.3 to 0.3
Outputs:
- weights_out: float32 [8, 4608, 2, 1024], P('replica', 'fsdp')
- first_out: float32 [8, 4608, 2, 1024], P('replica', 'fsdp')
- second_out: float32 [8, 4608, 2, 1024], P('replica', 'fsdp')
- anchor_out: float32 [4608, 1024], P('fsdp')
- momentum_out: float32 [4608, 1024], P('fsdp')
- input_grad: bfloat16 [8, 4096, 4608], P('replica', 'fsdp')
The draws below stay inside these ranges and needn't reach their ends.
All inputs are finite; a program needn't handle non-finite values.
Results may differ from the reference program's by a relative error of at most 0.0095.
Values may be sent and summed in bfloat16 or wider, within the bound.
No kernel may reach another device: no remote copies, remote signals or barrier semaphores. Data moves between devices by JAX's collectives and lax.ppermute only.
A program may use at most 128 MiB of HBM per device.

```python
import math
import jax
import jax.numpy as jnp
from jax import lax

D = 4608
TOK_DEV = 256
KV = 1024
TOKENS = 4096
N_REPLICA = 8
N_FSDP = 16


def shard_levels(key, extent, pieces, smallest, top_value):
    def one(dim, parts):
        steps = jax.random.uniform(jax.random.fold_in(jax.random.fold_in(key, 6), dim), (parts,), jnp.float32, smallest / len(pieces), top_value / len(pieces))
        return jnp.repeat(jnp.exp(steps), extent[dim] // parts).reshape((-1,) + (1,) * (len(extent) - dim - 1))

    gain = one(*pieces[0])
    for cut in pieces[1:]:
        gain = gain * one(*cut)
    return gain


def bell_draw(rng, shape, scale, bound, shards=(), dtype=jnp.bfloat16):
    factor_of = shard_levels(rng, shape, shards, -0.22, 0.18) if shards else 1.0
    result = jax.random.normal(rng, shape, jnp.float32) * scale * factor_of
    return jnp.minimum(jnp.maximum(result, -bound), bound).astype(dtype)


def setup_inputs(seed: int = 0) -> dict:
    splits = jax.random.split(jax.random.key(seed), 8)
    return {
        "activations": bell_draw(splits[0], (N_REPLICA, TOKENS, D), 1.0, 6.0, ((0, 8), (1, 16))),
        "cotangent": bell_draw(splits[1], (N_REPLICA, TOKENS, 2, KV), 0.03, 0.1796875, ((0, 8), (1, 16))),
        "weights": bell_draw(splits[2], (N_REPLICA, D, 2, KV), 0.1, 0.6, ((0, 8), (1, 16)), jnp.float32),
        "first_moment": bell_draw(splits[3], (N_REPLICA, D, 2, KV), 0.5, 3.0, ((0, 8), (1, 16)), jnp.float32),
        "second_moment": jnp.clip(jnp.exp(math.log(3.0) - 3.4011974 * jax.random.uniform(splits[4], (N_REPLICA, D, 2, KV), jnp.float32) ** shard_levels(splits[4], (N_REPLICA, D, 2, KV), ((0, 8), (1, 16)), -0.2, 0.2)), 0.1, 3.0),
        "anchor": bell_draw(splits[5], (D, KV), 0.1, 0.6, ((0, 16),), jnp.float32),
        "momentum": bell_draw(splits[6], (D, KV), 0.05, 0.3, ((0, 16),), jnp.float32),
    }


CORRECT_FIRST = 1.0 - 0.9 ** 8
CORRECT_SECOND = 1.0 - 0.95 ** 8

def one_replica(packed):
    inputs_rep, cot_rep, weight_rep, first_rep, second_rep = packed
    cot_flat = cot_rep.reshape(TOKENS, 2 * KV)
    input_blocks = inputs_rep.reshape(N_FSDP, TOK_DEV, D)
    cot_blocks = cot_flat.reshape(N_FSDP, TOK_DEV, 2 * KV)

    def accumulate(total, pair):
        block_part = jnp.dot(pair[0].T, pair[1], preferred_element_type=jnp.float32).astype(jnp.bfloat16)
        block_part = lax.optimization_barrier(block_part)
        return (total + block_part.astype(jnp.float32), None)
    gradient, _ = lax.scan(accumulate, jnp.zeros((D, 2 * KV), jnp.float32), (input_blocks, cot_blocks))
    gradient = gradient.reshape(D, 2, KV)
    weight_low = weight_rep.astype(jnp.bfloat16).reshape(D, 2 * KV)
    input_grad = lax.dot_general(cot_flat, weight_low, (((1,), (1,)), ((), ())), preferred_element_type=jnp.float32).astype(jnp.bfloat16)
    first_new = 0.9 * first_rep + 0.1 * gradient
    second_new = 0.95 * second_rep + 0.05 * gradient * gradient
    step_dir = first_new / CORRECT_FIRST / (jnp.sqrt(second_new / CORRECT_SECOND) + 1e-08)
    inner = weight_rep - 0.01 * (step_dir + 0.1 * weight_rep)
    return (inner, first_new, second_new, input_grad)

def reference(activations, cotangent, weights, first_moment, second_moment, anchor, momentum):
    inner, first_out, second_out, input_grad = lax.map(one_replica, (activations, cotangent, weights, first_moment, second_moment))
    selected = inner[:, :, 0, :]
    delta = anchor - lax.optimization_barrier(jnp.sum(selected, axis=0)) / N_REPLICA
    momentum_out = 0.9 * momentum + delta
    anchor_out = anchor - 0.7 * (delta + 0.9 * momentum_out)
    synced = jnp.broadcast_to(anchor_out[None, :, None, :], (N_REPLICA, D, 1, KV))
    weights_out = jnp.concatenate([synced, inner[:, :, 1:, :]], axis=2)
    return (weights_out, first_out, second_out, anchor_out, momentum_out, input_grad)
```

```python
import jax
import jax.numpy as jnp
import numpy as np
from jax import lax
from jax.sharding import Mesh
from jax.sharding import PartitionSpec as P

CORRECT_FIRST = 1.0 - 0.9**8
CORRECT_SECOND = 1.0 - 0.95**8
AXES = ("ylo", "z", "yhi", "x", "core")
SIZES = (2, 4, 2, 4, 2)
BF16 = jnp.bfloat16
F32 = jnp.float32


def shift(value, **steps):
    pairs = []
    for source in np.ndindex(*SIZES):
        target = [(s + steps.get(a, 0)) % n for s, a, n in zip(source, AXES, SIZES)]
        pairs.append(
            (int(np.ravel_multi_index(source, SIZES)), int(np.ravel_multi_index(target, SIZES)))
        )
    return lax.ppermute(value, AXES, pairs)


def dot(a, b, dims):
    return lax.dot_general(a, b, (dims, ((), ())), preferred_element_type=F32)


def half(x, which, axis):
    n = x.shape[axis] // 2
    return lax.dynamic_slice_in_dim(x, which * n, n, axis)


def shards(activations, cotangent, weights, first_moment, second_moment, anchor, momentum):
    acts = activations[0]
    tok, width = acts.shape
    weight_here = weights[0]
    rows = weight_here.shape[0]
    feat = weight_here.shape[2]
    h = lax.axis_index("yhi")
    c = lax.axis_index("core")
    x = lax.axis_index("x")
    cot = cotangent[0]
    cots = [cot[:, 0, :], cot[:, 1, :]]

    weight_low = weight_here.astype(BF16).reshape(rows, 2 * feat)
    w_all = lax.all_gather(weight_low, "x", axis=0, tiled=True)

    a_far = shift(half(acts, 1 - h, 1), yhi=1)
    c_far = [shift(t, yhi=1) for t in cots]
    a_two = jnp.concatenate([half(acts, h, 1), a_far], 0)

    def columns(v, core):
        v4 = v.reshape(2 * tok, 4, 2, rows)
        return lax.dynamic_index_in_dim(v4, core, 2, keepdims=False).reshape(2 * tok, 4 * rows)

    a_mine = columns(a_two, c)
    a_other = shift(columns(a_two, 1 - c), core=1)
    a_all = jnp.concatenate([a_mine, a_other], 0)
    c_two = [jnp.concatenate([n, f], 0) for n, f in zip(cots, c_far)]
    c_all = [jnp.concatenate([v, shift(v, core=1)], 0) for v in c_two]

    def block(v, i, lo, n):
        return lax.dynamic_slice_in_dim(v, lax.rem(i + 8, 4) * rows + lo, n, 0)

    hr = rows // 2

    def scatter(part):
        up = shift(block(part, x + 2, 0, hr).astype(BF16), x=1)
        down = shift(block(part, x - 2, hr, hr).astype(BF16), x=-1)
        to_up = jnp.concatenate(
            [block(part, x + 1, 0, hr) + up.astype(F32), block(part, x + 1, hr, hr)], 0
        ).astype(BF16)
        to_down = jnp.concatenate(
            [block(part, x - 1, 0, hr), block(part, x - 1, hr, hr) + down.astype(F32)], 0
        ).astype(BF16)
        return (
            block(part, x, 0, rows)
            + shift(to_up, x=1).astype(F32)
            + shift(to_down, x=-1).astype(F32)
        )

    grads = [scatter(dot(a_all, v, ((0,), (0,)))) for v in c_all]

    firsts, seconds, inners = [], [], []
    for f in range(2):
        g = grads[f]
        w = weight_here[:, f, :]
        m = 0.9 * first_moment[0, :, f, :] + 0.1 * g
        v = 0.95 * second_moment[0, :, f, :] + 0.05 * g * g
        step_dir = m / CORRECT_FIRST / (jnp.sqrt(v / CORRECT_SECOND) + 1e-08)
        firsts.append(m)
        seconds.append(v)
        inners.append(w - 0.01 * (step_dir + 0.1 * w))

    ylo = lax.axis_index("ylo")
    z = lax.axis_index("z")
    sel = inners[0]
    pair = half(sel, ylo, 0) + shift(half(sel, 1 - ylo, 0).astype(BF16), ylo=1).astype(F32)
    qr = rows // 8

    def quarter(i):
        return lax.dynamic_slice_in_dim(pair, lax.rem(i + 8, 4) * qr, qr, 0)

    total = quarter(z)
    for s in (1, -1, 2):
        total = total + shift(quarter(z + s).astype(BF16), z=s).astype(F32)
    mean = (total / 8).astype(BF16)
    back = jnp.zeros((rows // 2, feat), BF16)
    back = lax.dynamic_update_slice_in_dim(back, mean, z * qr, 0)
    for s in (1, -1, 2):
        back = lax.dynamic_update_slice_in_dim(
            back, shift(mean, z=s), lax.rem(z - s + 8, 4) * qr, 0
        )
    other = shift(back, ylo=1)
    low = lax.select(ylo == 0, back, other)
    high = lax.select(ylo == 0, other, back)
    mean_all = jnp.concatenate([low, high], 0).astype(F32)
    delta = anchor - mean_all
    momentum_out = 0.9 * momentum + delta
    anchor_out = anchor - 0.7 * (delta + 0.9 * momentum_out)

    cot_all = jnp.concatenate(c_all, 1)

    def ig(b):
        return dot(cot_all[b * tok : (b + 1) * tok], w_all, ((1,), (1,))).astype(BF16)

    far = shift(ig(1), yhi=1)
    far_other = shift(ig(3), yhi=1, core=1)
    near_other = shift(ig(2), core=1)
    near = ig(0)

    def order(a0, a1, bit):
        return lax.select(bit == 0, a0, a1), lax.select(bit == 0, a1, a0)

    n0, n1 = order(near, near_other, c)
    f0, f1 = order(far, far_other, c)
    h00, h10 = order(n0, f0, h)
    h01, h11 = order(n1, f1, h)

    def weave(p0, p1):
        return jnp.stack(
            [p0.reshape(tok, 4, rows), p1.reshape(tok, 4, rows)], 2
        ).reshape(tok, 8 * rows)

    input_grad = jnp.concatenate([weave(h00, h01), weave(h10, h11)], 1)

    weights_out = jnp.stack([anchor_out, inners[1]], 1)
    return (
        weights_out[None],
        jnp.stack(firsts, 1)[None],
        jnp.stack(seconds, 1)[None],
        anchor_out,
        momentum_out,
        input_grad[None],
    )


def solution(mesh):
    fine = Mesh(mesh.devices.reshape(SIZES), AXES)
    rep, fs = ("ylo", "z"), ("yhi", "x", "core")
    in_specs = (
        P(rep, fs, None),
        P(rep, fs, None, None),
        P(rep, fs, None, None),
        P(rep, fs, None, None),
        P(rep, fs, None, None),
        P(fs, None),
        P(fs, None),
    )
    out_specs = (
        P(rep, fs, None, None),
        P(rep, fs, None, None),
        P(rep, fs, None, None),
        P(fs, None),
        P(fs, None),
        P(rep, fs, None),
    )
    return jax.shard_map(shards, mesh=fine, in_specs=in_specs, out_specs=out_specs, check_vma=False)
```

```python
import functools

import jax
import jax.numpy as jnp
import numpy as np
from jax import lax
from jax.experimental import pallas as pl
from jax.experimental.pallas import tpu as pltpu
from jax.sharding import Mesh
from jax.sharding import PartitionSpec as P

CORRECT_FIRST = 1.0 - 0.9**8
CORRECT_SECOND = 1.0 - 0.95**8
AXES = ("ylo", "z", "yhi", "x", "core")
SIZES = (2, 4, 2, 4, 2)
BF16 = jnp.bfloat16
F32 = jnp.float32
ANY = pl.BlockSpec(memory_space=pl.ANY)
SCALARS = pl.BlockSpec(memory_space=pltpu.SMEM)
VMEM_BYTES = 48 * 1024 * 1024


def shift(value, **steps):
    pairs = []
    for source in np.ndindex(*SIZES):
        target = [(s + steps.get(a, 0)) % n for s, a, n in zip(source, AXES, SIZES)]
        pairs.append(
            (int(np.ravel_multi_index(source, SIZES)), int(np.ravel_multi_index(target, SIZES)))
        )
    return lax.ppermute(value, AXES, pairs)


def call(kernel, out_shape, inputs, in_specs, out_specs, scratch, flops=0, moved=0):
    return pl.pallas_call(
        kernel,
        out_shape=out_shape,
        in_specs=in_specs,
        out_specs=out_specs,
        scratch_shapes=scratch,
        compiler_params=pltpu.CompilerParams(vmem_limit_bytes=VMEM_BYTES),
        cost_estimate=pl.CostEstimate(flops=flops, bytes_accessed=moved, transcendentals=0),
    )(*inputs)


def far_half_kernel(place, acts, out, sem):
    n = out.shape[1]
    copy = pltpu.make_async_copy(
        acts.at[:, pl.ds(pl.multiple_of((1 - place[0]) * n, 128), n)], out, sem
    )
    copy.start()
    copy.wait()


def gradient_kernel(place, acts, a_far, c_own, c_far, mine, other, a_s, c_s, g_s, in_sem, out_sem):
    h, c = place[0], place[1]
    tok, wide = a_far.shape
    rows = mine.shape[1]
    copies = [
        pltpu.make_async_copy(
            acts.at[:, pl.ds(pl.multiple_of(h * wide, 128), wide)],
            a_s.at[pl.ds(0, tok)],
            in_sem.at[0],
        ),
        pltpu.make_async_copy(a_far, a_s.at[pl.ds(tok, tok)], in_sem.at[1]),
        pltpu.make_async_copy(c_own, c_s.at[pl.ds(0, tok)], in_sem.at[2]),
        pltpu.make_async_copy(c_far, c_s.at[pl.ds(tok, tok)], in_sem.at[3]),
    ]
    for copy in copies:
        copy.start()
    for copy in copies:
        copy.wait()
    tile = 256
    sent = 0
    for i in range(wide // tile):
        g_s[i * tile : (i + 1) * tile, :] = lax.dot_general(
            a_s[:, i * tile : (i + 1) * tile],
            c_s[...],
            (((0,), (0,)), ((), ())),
            preferred_element_type=F32,
        ).astype(BF16)
        while (sent + 1) * rows <= (i + 1) * tile:
            block = g_s.at[pl.ds(sent * rows, rows)]
            to, core = sent // 2, sent % 2

            @pl.when(c == core)
            def _(block=block, to=to, sent=sent):
                pltpu.make_async_copy(block, mine.at[to], out_sem.at[sent]).start()

            @pl.when(c != core)
            def _(block=block, to=to, sent=sent):
                pltpu.make_async_copy(block, other.at[to], out_sem.at[sent]).start()

            sent += 1
    for b in range(sent):
        pltpu.make_async_copy(
            g_s.at[pl.ds(b * rows, rows)], mine.at[b // 2], out_sem.at[b]
        ).wait()


def input_kernel(place, w0, wm, wp, w2a, w2b, k0, v0, k1, v1, out0, out1, w_s, sem):
    x = place[2]
    rows = w0.shape[0]
    part = rows // 2

    def at(step, lo, n):
        return w_s.at[pl.ds(pl.multiple_of(lax.rem(x + step, 4) * rows + lo, 16), n)]

    copies = [
        pltpu.make_async_copy(w0, at(0, 0, rows), sem.at[0]),
        pltpu.make_async_copy(wm, at(3, 0, rows), sem.at[1]),
        pltpu.make_async_copy(wp, at(1, 0, rows), sem.at[2]),
        pltpu.make_async_copy(w2a, at(2, 0, part), sem.at[3]),
        pltpu.make_async_copy(w2b, at(2, part, part), sem.at[4]),
    ]
    for copy in copies:
        copy.start()
    for copy in copies:
        copy.wait()
    feat = k0.shape[1]
    tile = 384
    for j in range(4 * rows // tile):
        wk = w_s[j * tile : (j + 1) * tile, :feat]
        wv = w_s[j * tile : (j + 1) * tile, feat:]
        for key, val, out in ((k0, v0, out0), (k1, v1, out1)):
            dims = (((1,), (1,)), ((), ()))
            acc = lax.dot_general(key[...], wk, dims, preferred_element_type=F32)
            acc += lax.dot_general(val[...], wv, dims, preferred_element_type=F32)
            out[:, j * tile : (j + 1) * tile] = acc.astype(BF16)


def shards(activations, cotangent, weights, first_moment, second_moment, anchor, momentum):
    acts = activations[0]
    tok, width = acts.shape
    weight_here = weights[0]
    rows = weight_here.shape[0]
    feat = weight_here.shape[2]
    ylo, z, h, x, c = [lax.axis_index(a) for a in AXES]
    place = jnp.stack([h, c, x]).astype(jnp.int32)
    cot = cotangent[0]
    cots = [cot[:, 0, :], cot[:, 1, :]]
    hr = rows // 2

    key_far = shift(cots[0], yhi=1)
    a_send = call(
        far_half_kernel,
        jax.ShapeDtypeStruct((tok, width // 2), BF16),
        (place, acts),
        [SCALARS, ANY],
        ANY,
        [pltpu.SemaphoreType.DMA],
        moved=2 * tok * width,
    )
    a_far = shift(a_send, yhi=1)
    val_far = shift(cots[1], yhi=1)
    fars = [key_far, val_far]

    w0 = weight_here.astype(BF16).reshape(rows, 2 * feat)
    wm = shift(w0, x=1)
    wp = shift(w0, x=-1)
    w2a = shift(wm[:hr], x=1)
    w2b = shift(wp[hr:], x=-1)

    def block(v, i, lo, n):
        return lax.dynamic_slice(v, (lax.rem(i + 8, 4), lo, 0), (1, n, feat))[0].astype(F32)

    def gradient(f):
        mine, other = call(
            gradient_kernel,
            [jax.ShapeDtypeStruct((4, rows, feat), BF16)] * 2,
            (place, acts, a_far, cots[f], fars[f]),
            [SCALARS, ANY, ANY, ANY, ANY],
            [ANY, ANY],
            [
                pltpu.VMEM((2 * tok, width // 2), BF16),
                pltpu.VMEM((2 * tok, feat), BF16),
                pltpu.VMEM((width // 2, feat), BF16),
                pltpu.SemaphoreType.DMA((4,)),
                pltpu.SemaphoreType.DMA((8,)),
            ],
            flops=2 * 2 * tok * width // 2 * feat,
            moved=12 * 2**20,
        )
        got = shift(other, core=1)

        def part(i, lo, n):
            return block(mine, i, lo, n) + block(got, i, lo, n)

        up = shift(part(x + 2, 0, hr).astype(BF16), x=1)
        down = shift(part(x - 2, hr, hr).astype(BF16), x=-1)
        to_up = jnp.concatenate(
            [part(x + 1, 0, hr) + up.astype(F32), part(x + 1, hr, hr)], 0
        ).astype(BF16)
        to_down = jnp.concatenate(
            [part(x - 1, 0, hr), part(x - 1, hr, hr) + down.astype(F32)], 0
        ).astype(BF16)
        return (
            part(x, 0, rows) + shift(to_up, x=1).astype(F32) + shift(to_down, x=-1).astype(F32)
        )

    grads = [gradient(0), gradient(1)]

    firsts, seconds, inners = [], [], []
    for f in range(2):
        g = grads[f]
        w = weight_here[:, f, :]
        m = 0.9 * first_moment[0, :, f, :] + 0.1 * g
        v = 0.95 * second_moment[0, :, f, :] + 0.05 * g * g
        step_dir = m / CORRECT_FIRST / (jnp.sqrt(v / CORRECT_SECOND) + 1e-08)
        firsts.append(m)
        seconds.append(v)
        inners.append(w - 0.01 * (step_dir + 0.1 * w))

    sel = inners[0]
    qc = feat // 4

    def quarter(i):
        return lax.dynamic_slice_in_dim(sel, lax.rem(i + 8, 4) * qc, qc, 1)

    total = quarter(z)
    for s in (1, -1, 2):
        total = total + shift(quarter(z + s).astype(BF16), z=s).astype(F32)
    total = lax.reduce_precision(total, 8, 7)
    total = total + shift(total.astype(BF16), ylo=1).astype(F32)
    mean = (total / 8).astype(BF16)
    ring = jnp.stack([mean, shift(mean, z=-1), shift(mean, z=2), shift(mean, z=1)])
    mean_all = jnp.concatenate(
        [lax.dynamic_index_in_dim(ring, lax.rem(q - z + 4, 4), 0, keepdims=False) for q in range(4)],
        1,
    ).astype(F32)
    delta = anchor - mean_all
    momentum_out = 0.9 * momentum + delta
    anchor_out = anchor - 0.7 * (delta + 0.9 * momentum_out)

    twos = [jnp.concatenate([n, f], 0) for n, f in zip(cots, fars)]
    oths = [shift(t, core=1) for t in twos]

    def input_part(b):
        lo, hi = b * tok, (b + 1) * tok
        return call(
            input_kernel,
            [jax.ShapeDtypeStruct((tok, 4 * rows), BF16)] * 2,
            (place, w0, wm, wp, w2a, w2b)
            + (twos[0][lo:hi], twos[1][lo:hi], oths[0][lo:hi], oths[1][lo:hi]),
            [SCALARS, ANY, ANY, ANY, ANY, ANY] + [pl.BlockSpec(memory_space=pltpu.VMEM)] * 4,
            [pl.BlockSpec(memory_space=pltpu.VMEM)] * 2,
            [pltpu.VMEM((4 * rows, 2 * feat), BF16), pltpu.SemaphoreType.DMA((5,))],
            flops=2 * 2 * tok * 4 * rows * 2 * feat,
            moved=8 * 2**20,
        )

    out_far, out_far_other = input_part(1)
    far = shift(out_far, yhi=1)
    far_other = shift(out_far_other, yhi=1, core=1)
    near, out_near_other = input_part(0)
    near_other = shift(out_near_other, core=1)

    def order(a0, a1, bit):
        return lax.select(bit == 0, a0, a1), lax.select(bit == 0, a1, a0)

    n0, n1 = order(near, near_other, c)
    f0, f1 = order(far, far_other, c)
    h00, h10 = order(n0, f0, h)
    h01, h11 = order(n1, f1, h)

    def weave(p0, p1):
        return jnp.stack(
            [p0.reshape(tok, 4, rows), p1.reshape(tok, 4, rows)], 2
        ).reshape(tok, 8 * rows)

    input_grad = jnp.concatenate([weave(h00, h01), weave(h10, h11)], 1)

    weights_out = jnp.stack([anchor_out, inners[1]], 1)
    return (
        weights_out[None],
        jnp.stack(firsts, 1)[None],
        jnp.stack(seconds, 1)[None],
        anchor_out,
        momentum_out,
        input_grad[None],
    )


def solution(mesh):
    fine = Mesh(mesh.devices.reshape(SIZES), AXES)
    rep, fs = ("ylo", "z"), ("yhi", "x", "core")
    in_specs = (
        P(rep, fs, None),
        P(rep, fs, None, None),
        P(rep, fs, None, None),
        P(rep, fs, None, None),
        P(rep, fs, None, None),
        P(fs, None),
        P(fs, None),
    )
    out_specs = (
        P(rep, fs, None, None),
        P(rep, fs, None, None),
        P(rep, fs, None, None),
        P(fs, None),
        P(fs, None),
        P(rep, fs, None),
    )
    return jax.shard_map(shards, mesh=fine, in_specs=in_specs, out_specs=out_specs, check_vma=False)
```

```python
import jax
import jax.numpy as jnp
import numpy as np
from jax import lax
from jax.experimental import pallas as pl
from jax.experimental.pallas import tpu as pltpu
from jax.sharding import Mesh
from jax.sharding import PartitionSpec as P

CORRECT_FIRST = 1.0 - 0.9**8
CORRECT_SECOND = 1.0 - 0.95**8
AXES = ("ylo", "z", "yhi", "x", "core")
SIZES = (2, 4, 2, 4, 2)
BF16 = jnp.bfloat16
F32 = jnp.float32
ANY = pl.BlockSpec(memory_space=pl.ANY)
VMEM_BYTES = 48 * 1024 * 1024


def shift(value, **steps):
    pairs = []
    for source in np.ndindex(*SIZES):
        target = [(s + steps.get(a, 0)) % n for s, a, n in zip(source, AXES, SIZES)]
        pairs.append(
            (int(np.ravel_multi_index(source, SIZES)), int(np.ravel_multi_index(target, SIZES)))
        )
    return lax.ppermute(value, AXES, pairs)


def call(kernel, out_shape, place, inputs, in_specs, out_specs, scratch=(), grid=(1,), flops=0, moved=0):
    return pl.pallas_call(
        kernel,
        out_shape=out_shape,
        grid_spec=pltpu.PrefetchScalarGridSpec(
            num_scalar_prefetch=1,
            grid=grid,
            in_specs=in_specs,
            out_specs=out_specs,
            scratch_shapes=list(scratch),
        ),
        compiler_params=pltpu.CompilerParams(vmem_limit_bytes=VMEM_BYTES),
        cost_estimate=pl.CostEstimate(flops=flops, bytes_accessed=moved, transcendentals=0),
    )(place, *inputs)


def after(value, *others):
    return lax.optimization_barrier((value, *others))[0]


def shape(dims, dtype=BF16):
    return jax.ShapeDtypeStruct(dims, dtype)


def far_half_kernel(place, acts, out, sem):
    n = out.shape[1]
    copy = pltpu.make_async_copy(
        acts.at[:, pl.ds(pl.multiple_of((1 - place[0]) * n, 128), n)], out, sem
    )
    copy.start()
    copy.wait()


def gradient_kernel(
    place, acts, a_far, c_own, c_far, mine, other, both, a_s, c_s, g_s, in_sem, out_sem, both_sem
):
    h, c = place[0], place[1]
    tok, wide = a_far.shape
    rows = mine.shape[1]
    copies = [
        pltpu.make_async_copy(
            acts.at[:, pl.ds(pl.multiple_of(h * wide, 128), wide)],
            a_s.at[pl.ds(0, tok)],
            in_sem.at[0],
        ),
        pltpu.make_async_copy(a_far, a_s.at[pl.ds(tok, tok)], in_sem.at[1]),
        pltpu.make_async_copy(c_own, c_s.at[pl.ds(0, tok)], in_sem.at[2]),
        pltpu.make_async_copy(c_far, c_s.at[pl.ds(tok, tok)], in_sem.at[3]),
    ]
    for copy in copies:
        copy.start()
    for copy in copies:
        copy.wait()
    keep = pltpu.make_async_copy(c_s, both, both_sem)
    keep.start()
    tile = 256
    sent = 0
    for i in range(wide // tile):
        g_s[i * tile : (i + 1) * tile, :] = lax.dot_general(
            a_s[:, i * tile : (i + 1) * tile],
            c_s[...],
            (((0,), (0,)), ((), ())),
            preferred_element_type=F32,
        ).astype(BF16)
        while (sent + 1) * rows <= (i + 1) * tile:
            block = g_s.at[pl.ds(sent * rows, rows)]
            to, core = sent // 2, sent % 2

            @pl.when(c == core)
            def _(block=block, to=to, sent=sent):
                pltpu.make_async_copy(block, mine.at[to], out_sem.at[sent]).start()

            @pl.when(c != core)
            def _(block=block, to=to, sent=sent):
                pltpu.make_async_copy(block, other.at[to], out_sem.at[sent]).start()

            sent += 1
    for b in range(sent):
        pltpu.make_async_copy(
            g_s.at[pl.ds(b * rows, rows)], mine.at[b // 2], out_sem.at[b]
        ).wait()
    keep.wait()


def block_sum(mine, got):
    return mine[0].astype(F32) + got[0].astype(F32)


def first_hop_kernel(place, mine, got, up, down):
    part = block_sum(mine, got).astype(BF16)
    n = up.shape[0]
    up[...] = part[:n]
    down[...] = part[n:]


def second_hop_kernel(place, mine_up, got_up, mine_down, got_down, up, down, to_up, to_down):
    n = up.shape[0]
    part = block_sum(mine_up, got_up)
    to_up[:n] = (part[:n] + up[...].astype(F32)).astype(BF16)
    to_up[n:] = part[n:].astype(BF16)
    part = block_sum(mine_down, got_down)
    to_down[:n] = part[:n].astype(BF16)
    to_down[n:] = (part[n:] + down[...].astype(F32)).astype(BF16)


def owned_sum(mine, got, up, down):
    return block_sum(mine, got) + up[...].astype(F32) + down[...].astype(F32)


def adamw(w, m, v, g):
    m = 0.9 * m + 0.1 * g
    v = 0.95 * v + 0.05 * g * g
    step_dir = m / CORRECT_FIRST / (jnp.sqrt(v / CORRECT_SECOND) + 1e-08)
    return m, v, w - 0.01 * (step_dir + 0.1 * w)


def selected_kernel(place, w, m, v, mine, got, up, down, own, s1, s2, s3, sel):
    g = owned_sum(mine, got, up, down)
    sel[...] = adamw(w[:, 0, :], m[:, 0, :], v[:, 0, :], g)[2]
    n = own.shape[1]
    for step, out in ((0, own), (1, s1), (2, s2), (3, s3)):
        start = pl.multiple_of(lax.rem(place[3] + step, 4) * n, 128)
        out[...] = sel[:, pl.ds(start, n)].astype(out.dtype)


def moments_kernel(place, w, m, v, *rest):
    parts, (first, second, inner) = (rest[:4], rest[4:8]), rest[8:]
    for f in range(2):
        g = owned_sum(*parts[f])
        m_new, v_new, inner_new = adamw(w[:, f, :], m[:, f, :], v[:, f, :], g)
        first[:, f, :] = m_new
        second[:, f, :] = v_new
    inner[...] = inner_new


def outer_kernel(place, m0, m1, m2, m3, anchor, momentum, inner, weights, anchor_new, momentum_new, mean):
    n = m0.shape[1]
    for step, part in enumerate((m0, m1, m2, m3)):
        start = pl.multiple_of(lax.rem(place[3] + step, 4) * n, 128)
        mean[:, pl.ds(start, n)] = part[...].astype(F32)
    delta = anchor[...] - mean[...]
    moved = 0.9 * momentum[...] + delta
    synced = anchor[...] - 0.7 * (delta + 0.9 * moved)
    momentum_new[...] = moved
    anchor_new[...] = synced
    weights[:, 0, :] = synced
    weights[:, 1, :] = inner[...]


def weave_kernel(place, near, far, near_other, far_other, out, held):
    h, c = place[0], place[1]
    held[2 * h + c] = near[...]
    held[2 * (1 - h) + c] = far[...]
    held[2 * h + (1 - c)] = near_other[...]
    held[2 * (1 - h) + (1 - c)] = far_other[...]
    rows = near.shape[1] // 4
    for yhi in range(2):
        for to in range(4):
            for core in range(2):
                b = (yhi * 4 + to) * 2 + core
                out[:, b * rows : (b + 1) * rows] = held[
                    2 * yhi + core, :, to * rows : (to + 1) * rows
                ]


def input_kernel(place, w0, wm, wp, w2a, w2b, k0, v0, k1, v1, out0, out1, w_s, sem):
    x = place[2]
    rows = w0.shape[0]
    part = rows // 2

    def at(step, lo, n):
        return w_s.at[pl.ds(pl.multiple_of(lax.rem(x + step, 4) * rows + lo, 16), n)]

    copies = [
        pltpu.make_async_copy(w0, at(0, 0, rows), sem.at[0]),
        pltpu.make_async_copy(wm, at(3, 0, rows), sem.at[1]),
        pltpu.make_async_copy(wp, at(1, 0, rows), sem.at[2]),
        pltpu.make_async_copy(w2a, at(2, 0, part), sem.at[3]),
        pltpu.make_async_copy(w2b, at(2, part, part), sem.at[4]),
    ]
    for copy in copies:
        copy.start()
    for copy in copies:
        copy.wait()
    feat = k0.shape[1]
    tile = 384
    for j in range(4 * rows // tile):
        wk = w_s[j * tile : (j + 1) * tile, :feat]
        wv = w_s[j * tile : (j + 1) * tile, feat:]
        for key, val, out in ((k0, v0, out0), (k1, v1, out1)):
            dims = (((1,), (1,)), ((), ()))
            acc = lax.dot_general(key[...], wk, dims, preferred_element_type=F32)
            acc += lax.dot_general(val[...], wv, dims, preferred_element_type=F32)
            out[:, j * tile : (j + 1) * tile] = acc.astype(BF16)


def shards(activations, cotangent, weights, first_moment, second_moment, anchor, momentum):
    acts = activations[0]
    tok, width = acts.shape
    weight_here = weights[0]
    rows = weight_here.shape[0]
    feat = weight_here.shape[2]
    ylo, z, h, x, c = [lax.axis_index(a) for a in AXES]
    place = jnp.stack([h, c, x, z]).astype(jnp.int32)
    hr = rows // 2

    a_send = call(
        far_half_kernel,
        shape((tok, width // 2)),
        place,
        (acts,),
        [ANY],
        ANY,
        [pltpu.SemaphoreType.DMA],
        moved=2 * tok * width,
    )
    a_far = shift(a_send, yhi=1)
    w0 = weight_here.astype(BF16).reshape(rows, 2 * feat)
    wm = shift(w0, x=1)
    wp = shift(w0, x=-1)
    cot = after(cotangent, w0, a_send)[0]
    cots = [cot[:, 0, :], cot[:, 1, :]]
    fars = [shift(t, yhi=1) for t in cots]
    w2a = shift(wm[:hr], x=1)
    w2b = shift(wp[hr:], x=-1)

    def partial(f):
        return call(
            gradient_kernel,
            [shape((4, rows, feat))] * 2 + [shape((2 * tok, feat))],
            place,
            (acts, a_far, cots[f], fars[f]),
            [ANY] * 4,
            [ANY] * 3,
            [
                pltpu.VMEM((2 * tok, width // 2), BF16),
                pltpu.VMEM((2 * tok, feat), BF16),
                pltpu.VMEM((width // 2, feat), BF16),
                pltpu.SemaphoreType.DMA((4,)),
                pltpu.SemaphoreType.DMA((8,)),
                pltpu.SemaphoreType.DMA,
            ],
            flops=2 * 2 * tok * width // 2 * feat,
            moved=12 * 2**20,
        )

    def block(step):
        return pl.BlockSpec((1, rows, feat), lambda i, place: (lax.rem(place[2] + step, 4), 0, 0))

    def whole(*dims):
        return pl.BlockSpec(dims, lambda i, place: (0,) * len(dims))

    def first_hop(mine, got):
        up, down = call(
            first_hop_kernel,
            [shape((hr, feat))] * 2,
            place,
            (mine, got),
            [block(2)] * 2,
            [whole(hr, feat)] * 2,
            moved=2**21,
        )
        return up, down

    def second_hop(mine, got, up, down):
        return call(
            second_hop_kernel,
            [shape((rows, feat))] * 2,
            place,
            (mine, got, mine, got, up, down),
            [block(1), block(1), block(3), block(3), whole(hr, feat), whole(hr, feat)],
            [whole(rows, feat)] * 2,
            moved=2**22,
        )

    mine0, other0, both0 = partial(0)
    got0 = shift(other0, core=1)
    oth0 = shift(both0, core=1)
    mine1, other1, both1 = partial(1)
    got1 = shift(other1, core=1)
    oth1 = shift(both1, core=1)
    up0, down0 = first_hop(mine0, got0)
    up0r, down0r = shift(up0, x=1), shift(down0, x=-1)
    up1, down1 = first_hop(mine1, got1)
    up1r, down1r = shift(up1, x=1), shift(down1, x=-1)
    to_up0, to_down0 = second_hop(mine0, got0, up0r, down0r)
    from_down0, from_up0 = shift(to_up0, x=1), shift(to_down0, x=-1)
    to_up1, to_down1 = second_hop(mine1, got1, up1r, down1r)
    from_down1, from_up1 = shift(to_up1, x=1), shift(to_down1, x=-1)

    def input_part(b, first):
        tokens = pl.BlockSpec((tok, feat), lambda i, place: (b, 0))
        return call(
            input_kernel,
            [shape((tok, 4 * rows))] * 2,
            place,
            (first, wm, wp, w2a, w2b, both0, both1, oth0, oth1),
            [ANY] * 5 + [tokens] * 4,
            [whole(tok, 4 * rows)] * 2,
            [pltpu.VMEM((4 * rows, 2 * feat), BF16), pltpu.SemaphoreType.DMA((5,))],
            flops=2 * 2 * tok * 4 * rows * 2 * feat,
            moved=8 * 2**20,
        )

    out_far, out_far_other = input_part(1, after(w0, up0, up1))
    far = shift(out_far, yhi=1)
    far_other = shift(out_far_other, yhi=1, core=1)
    near, out_near_other = input_part(0, after(w0, to_up0, to_up1, out_far))
    near_other = shift(out_near_other, core=1)

    half_rows = pl.BlockSpec((hr, feat), lambda i, place: (i, 0))
    half_both = pl.BlockSpec((hr, 2, feat), lambda i, place: (i, 0, 0))
    half_own = pl.BlockSpec((1, hr, feat), lambda i, place: (place[2], i, 0))
    qc = feat // 4
    half_quarter = pl.BlockSpec((hr, qc), lambda i, place: (i, 0))
    sums0 = (mine0, got0, from_down0, from_up0)
    sums1 = (mine1, got1, from_down1, from_up1)
    sum_specs = [half_own, half_own, half_rows, half_rows]
    own, s1, s2, s3 = call(
        selected_kernel,
        [shape((rows, qc), F32)] + [shape((rows, qc))] * 3,
        place,
        (weight_here, first_moment[0], second_moment[0], *sums0),
        [half_both] * 3 + sum_specs,
        [half_quarter] * 4,
        [pltpu.VMEM((hr, feat), F32)],
        grid=(2,),
        moved=10 * 2**20,
    )
    total = own
    for s, part in ((1, s1), (2, s2), (-1, s3)):
        total = total + shift(part, z=s).astype(F32)
    total = lax.reduce_precision(total, 8, 7)
    total = total + shift(total.astype(BF16), ylo=1).astype(F32)
    mean = (total / 8).astype(BF16)
    means = (mean, shift(mean, z=-1), shift(mean, z=2), shift(mean, z=1))
    first_out, second_out, inner = call(
        moments_kernel,
        [shape((rows, 2, feat), F32)] * 2 + [shape((rows, feat), F32)],
        place,
        (weight_here, first_moment[0], second_moment[0], *sums0, *sums1),
        [half_both] * 3 + sum_specs * 2,
        [half_both] * 2 + [half_rows],
        grid=(2,),
        moved=16 * 2**20,
    )
    weights_out, anchor_out, momentum_out = call(
        outer_kernel,
        [shape((rows, 2, feat), F32)] + [shape((rows, feat), F32)] * 2,
        place,
        (*means, anchor, momentum, inner),
        [half_quarter] * 4 + [half_rows] * 3,
        [half_both] + [half_rows] * 2,
        [pltpu.VMEM((hr, feat), F32)],
        grid=(2,),
        moved=9 * 2**20,
    )

    tile = 64
    strip = pl.BlockSpec((tile, 4 * rows), lambda i, place: (i, 0))
    input_grad = call(
        weave_kernel,
        shape((tok, width)),
        place,
        (near, far, near_other, far_other),
        [strip] * 4,
        pl.BlockSpec((tile, width), lambda i, place: (i, 0)),
        [pltpu.VMEM((4, tile, 4 * rows), BF16)],
        grid=(tok // tile,),
        moved=5 * 2**20,
    )
    return (
        weights_out[None],
        first_out[None],
        second_out[None],
        anchor_out,
        momentum_out,
        input_grad[None],
    )


def solution(mesh):
    fine = Mesh(mesh.devices.reshape(SIZES), AXES)
    rep, fs = ("ylo", "z"), ("yhi", "x", "core")
    in_specs = (
        P(rep, fs, None),
        P(rep, fs, None, None),
        P(rep, fs, None, None),
        P(rep, fs, None, None),
        P(rep, fs, None, None),
        P(fs, None),
        P(fs, None),
    )
    out_specs = (
        P(rep, fs, None, None),
        P(rep, fs, None, None),
        P(rep, fs, None, None),
        P(fs, None),
        P(fs, None),
        P(rep, fs, None),
    )
    return jax.shard_map(shards, mesh=fine, in_specs=in_specs, out_specs=out_specs, check_vma=False)
```

```python
import jax
import jax.numpy as jnp
import numpy as np
from jax import lax
from jax.experimental import pallas as pl
from jax.experimental.pallas import tpu as pltpu
from jax.sharding import Mesh
from jax.sharding import PartitionSpec as P

CORRECT_FIRST = 1.0 - 0.9**8
CORRECT_SECOND = 1.0 - 0.95**8
AXES = ("ylo", "z", "yhi", "x", "core")
SIZES = (2, 4, 2, 4, 2)
BF16 = jnp.bfloat16
F32 = jnp.float32
ANY = pl.BlockSpec(memory_space=pl.ANY)
HBM = pl.BlockSpec(memory_space=pltpu.HBM)
WEIGHT = 50


def shift(value, **steps):
    pairs = []
    for source in np.ndindex(*SIZES):
        target = [(s + steps.get(a, 0)) % n for s, a, n in zip(source, AXES, SIZES)]
        pairs.append(
            (int(np.ravel_multi_index(source, SIZES)), int(np.ravel_multi_index(target, SIZES)))
        )
    return lax.ppermute(value, AXES, pairs)


def call(
    kernel, out_shape, place, inputs, in_specs, out_specs, scratch=(), grid=(1,), flops=0, moved=0, weight=0, alias=None, vmem=12
):
    return pl.pallas_call(
        kernel,
        out_shape=out_shape,
        grid_spec=pltpu.PrefetchScalarGridSpec(
            num_scalar_prefetch=1,
            grid=grid,
            in_specs=in_specs,
            out_specs=out_specs,
            scratch_shapes=list(scratch),
        ),
        compiler_params=pltpu.CompilerParams(vmem_limit_bytes=vmem * 2**20),
        input_output_aliases=alias or {},
        cost_estimate=pl.CostEstimate(flops=weight * 10**9, bytes_accessed=weight * 10**7, transcendentals=0),
    )(place, *inputs)


def after(value, *others):
    return lax.optimization_barrier((value, *others))[0]


def shape(dims, dtype=BF16):
    return jax.ShapeDtypeStruct(dims, dtype)


def far_half_kernel(place, acts, out, sem):
    n = out.shape[1]
    copy = pltpu.make_async_copy(
        acts.at[:, pl.ds(pl.multiple_of((1 - place[0]) * n, 128), n)], out, sem
    )
    copy.start()
    copy.wait()


def stack_kernel(place, *refs):
    out = refs[-1]
    n = 0
    for ref in refs[:-1]:
        out[n : n + ref.shape[0]] = ref[...]
        n += ref.shape[0]


def gradient_kernel(place, acts, a_far, c_own, c_far, mine, other, a_s, c_s, g_s, in_sem, out_sem):
    h, c = place[0], place[1]
    tok, wide = a_far.shape
    rows = mine.shape[1]
    copies = [
        pltpu.make_async_copy(
            acts.at[:, pl.ds(pl.multiple_of(h * wide, 128), wide)],
            a_s.at[pl.ds(0, tok)],
            in_sem.at[0],
        ),
        pltpu.make_async_copy(a_far, a_s.at[pl.ds(tok, tok)], in_sem.at[1]),
        pltpu.make_async_copy(c_own, c_s.at[pl.ds(0, tok)], in_sem.at[2]),
        pltpu.make_async_copy(c_far, c_s.at[pl.ds(tok, tok)], in_sem.at[3]),
    ]
    for copy in copies:
        copy.start()
    for copy in copies:
        copy.wait()
    tile = 256
    sends = []
    for i in range(wide // tile):
        cols = slice(i * tile, (i + 1) * tile)
        g_s[cols, :] = lax.dot_general(
            a_s[:, cols], c_s[...], (((0,), (0,)), ((), ())), preferred_element_type=F32
        ).astype(BF16)
        ready = {4: (0, 1), 8: (2, 3)}.get(i, ())
        for core, out in ((1 - c, other), (c, mine)):
            for to in ready:
                start = pl.multiple_of((2 * to + core) * rows, 16)
                sends.append(
                    pltpu.make_async_copy(
                        g_s.at[pl.ds(start, rows)], out.at[to], out_sem.at[len(sends)]
                    )
                )
                sends[-1].start()
    for send in sends:
        send.wait()


def rounded_kernel(place, w, w_low, w_key):
    n = w.shape[2]
    key = w[:, 0, :]
    w_key[...] = key
    w_low[:, :n] = key.astype(BF16)
    w_low[:, n:] = w[:, 1, :].astype(BF16)


def planes_kernel(place, m, v, m_key, v_key):
    m_key[...] = m[:, 0, :]
    v_key[...] = v[:, 0, :]


def block_sum(mine, got):
    return mine[0].astype(F32) + got[0].astype(F32)


def first_hop_kernel(place, mine, got, up, down):
    part = block_sum(mine, got).astype(BF16)
    n = up.shape[0]
    up[...] = part[:n]
    down[...] = part[n:]


def second_hop_kernel(place, mine_up, got_up, mine_down, got_down, up, down, to_up, to_down):
    n = up.shape[0]
    part = block_sum(mine_up, got_up)
    to_up[:n] = (part[:n] + up[...].astype(F32)).astype(BF16)
    to_up[n:] = part[n:].astype(BF16)
    part = block_sum(mine_down, got_down)
    to_down[:n] = part[:n].astype(BF16)
    to_down[n:] = (part[n:] + down[...].astype(F32)).astype(BF16)


def owned_sum(mine, got, up, down):
    return block_sum(mine, got) + up[...].astype(F32) + down[...].astype(F32)


def adamw(w, m, v, g):
    m = 0.9 * m + 0.1 * g
    v = 0.95 * v + 0.05 * g * g
    step_dir = m / CORRECT_FIRST / (jnp.sqrt(v / CORRECT_SECOND) + 1e-08)
    return m, v, w - 0.01 * (step_dir + 0.1 * w)


def selected_kernel(place, w, m, v, mine, got, up, down, own, s1, s2, s3, sel):
    g = owned_sum(mine, got, up, down)
    sel[...] = adamw(w[...], m[...], v[...], g)[2]
    n = own.shape[1]
    for step, out in ((0, own), (1, s1), (2, s2), (3, s3)):
        start = pl.multiple_of(lax.rem(place[3] + step, 4) * n, 128)
        out[...] = sel[:, pl.ds(start, n)].astype(out.dtype)


def moments_kernel(place, w, m, v, *rest):
    parts, (first, second, inner) = (rest[:4], rest[4:8]), rest[8:]
    for f in range(2):
        g = owned_sum(*parts[f])
        m_new, v_new, inner_new = adamw(w[:, f, :], m[:, f, :], v[:, f, :], g)
        first[:, f, :] = m_new
        second[:, f, :] = v_new
    inner[...] = inner_new


def outer_kernel(place, m0, m1, m2, m3, anchor, momentum, inner, weights, anchor_new, momentum_new, mean):
    n = m0.shape[1]
    for step, part in enumerate((m0, m1, m2, m3)):
        start = pl.multiple_of(lax.rem(place[3] + step, 4) * n, 128)
        mean[:, pl.ds(start, n)] = part[...].astype(F32)
    delta = anchor[...] - mean[...]
    moved = 0.9 * momentum[...] + delta
    synced = anchor[...] - 0.7 * (delta + 0.9 * moved)
    momentum_new[...] = moved
    anchor_new[...] = synced
    weights[:, 0, :] = synced
    weights[:, 1, :] = inner[...]


def far_columns_kernel(place, far, near, out):
    out[...] = far[...]


def input_kernel(
    place, w013, w2a, w2b, v013, v2, k_near, v_near, k_far, v_far, near, far, w_s, c_s, o_s, sem, out_sem
):
    h, c, x = place[0], place[1], place[2]
    rows, feat = v2.shape[0], k_near.shape[1]
    part = w2a.shape[0]
    tok, wide = far.shape
    pieces = []
    for core, triple in ((c, w013), (1 - c, v013)):
        for n, step in enumerate((0, 1, 3)):
            pieces.append((core, step, 0, triple, n * rows, rows))
    pieces += [(c, 2, 0, w2a, 0, part), (c, 2, part, w2b, 0, part), (1 - c, 2, 0, v2, 0, rows)]
    copies = [[], []]
    for f in range(2):
        for core, step, low, piece, first, n in pieces:
            start = (2 * lax.rem(x + step, 4) + core) * rows + low
            copies[f].append(
                pltpu.make_async_copy(
                    piece.at[pl.ds(first, n), pl.ds(f * feat, feat)],
                    w_s.at[f, pl.ds(pl.multiple_of(start, 16), n)],
                    sem.at[9 * f + len(copies[f])],
                )
            )
    for n, tokens in enumerate((k_far, k_near, v_far, v_near)):
        copies[n // 2].append(
            pltpu.make_async_copy(
                tokens, c_s.at[n // 2, pl.ds(n % 2 * tok, tok)], sem.at[18 + n]
            )
        )
    for copy in copies[0] + copies[1]:
        copy.start()
    for copy in copies[0] + copies[1]:
        copy.wait()
    tile = 384
    dims = (((1,), (1,)), ((), ()))
    sends = []
    for j in range(wide // tile):
        cols = slice(j * tile, (j + 1) * tile)
        acc = lax.dot_general(c_s[0], w_s[0, cols, :], dims, preferred_element_type=F32)
        acc += lax.dot_general(c_s[1], w_s[1, cols, :], dims, preferred_element_type=F32)
        o_s[:, cols] = acc.astype(BF16)
        for b, (out, base) in enumerate(((far, 0), (near, h * wide))):
            sends.append(
                pltpu.make_async_copy(
                    o_s.at[pl.ds(b * tok, tok), pl.ds(j * tile, tile)],
                    out.at[:, pl.ds(pl.multiple_of(base + j * tile, 128), tile)],
                    out_sem.at[len(sends)],
                )
            )
            sends[-1].start()
    for send in sends:
        send.wait()


def shards(activations, cotangent, weights, first_moment, second_moment, anchor, momentum):
    acts = activations[0]
    tok, width = acts.shape
    weight_here = weights[0]
    rows = weight_here.shape[0]
    feat = weight_here.shape[2]
    ylo, z, h, x, c = [lax.axis_index(a) for a in AXES]
    place = jnp.stack([h, c, x, z]).astype(jnp.int32)
    hr = rows // 2

    def whole(*dims):
        return pl.BlockSpec(dims, lambda i, place: (0,) * len(dims))

    half_rows = pl.BlockSpec((hr, feat), lambda i, place: (i, 0))
    half_both = pl.BlockSpec((hr, 2, feat), lambda i, place: (i, 0, 0))
    a_send = call(
        far_half_kernel,
        shape((tok, width // 2)),
        place,
        (acts,),
        [ANY],
        ANY,
        [pltpu.SemaphoreType.DMA],
        moved=2 * tok * width,
    )
    a_far = shift(a_send, yhi=1)
    w0, w_key = call(
        rounded_kernel,
        [shape((rows, 2 * feat)), shape((rows, feat), F32)],
        place,
        (after(weight_here, a_send),),
        [half_both],
        [pl.BlockSpec((hr, 2 * feat), lambda i, place: (i, 0)), half_rows],
        grid=(2,),
        moved=5 * 2**20,
        weight=WEIGHT,
    )
    w1, w3 = shift(w0, x=-1), shift(w0, x=1)
    cot = after(cotangent, w0, a_send)[0]
    key, val = cot[:, 0, :], cot[:, 1, :]
    key_far = shift(key, yhi=1)

    m_key, v_key = call(
        planes_kernel,
        [shape((rows, feat), F32)] * 2,
        place,
        (after(first_moment, key)[0], second_moment[0]),
        [half_both] * 2,
        [half_rows] * 2,
        grid=(2,),
        moved=7 * 2**20,
        weight=WEIGHT,
    )
    planes = (w_key, m_key, v_key)
    val_far = shift(after(val, m_key), yhi=1)

    def partial(a, c_own, c_far):
        return call(
            gradient_kernel,
            [shape((4, rows, feat))] * 2,
            place,
            (acts, a, c_own, c_far),
            [HBM] * 4,
            [HBM] * 2,
            [
                pltpu.VMEM((2 * tok, width // 2), BF16),
                pltpu.VMEM((2 * tok, feat), BF16),
                pltpu.VMEM((width // 2, feat), BF16),
                pltpu.SemaphoreType.DMA((4,)),
                pltpu.SemaphoreType.DMA((8,)),
            ],
            flops=2 * tok * width * feat,
            moved=12 * 2**20,
            weight=WEIGHT,
            vmem=16,
        )

    def block(step):
        return pl.BlockSpec((1, rows, feat), lambda i, place: (lax.rem(place[2] + step, 4), 0, 0))

    def first_hop(mine, got):
        up, down = call(
            first_hop_kernel,
            [shape((hr, feat))] * 2,
            place,
            (mine, got),
            [block(2)] * 2,
            [whole(hr, feat)] * 2,
            moved=2**21,
        )
        return up, down

    def second_hop(mine, got, up, down, weight=0):
        return call(
            second_hop_kernel,
            [shape((rows, feat))] * 2,
            place,
            (mine, got, mine, got, up, down),
            [block(1), block(1), block(3), block(3), whole(hr, feat), whole(hr, feat)],
            [whole(rows, feat)] * 2,
            moved=2**22,
            weight=weight,
        )

    a_far, w1, w3, planes = lax.optimization_barrier((a_far, w1, w3, planes))
    def stack(*parts):
        total = sum(p.shape[0] for p in parts)
        return call(
            stack_kernel,
            shape((total, 2 * feat)),
            place,
            parts,
            [whole(*p.shape) for p in parts],
            whole(total, 2 * feat),
            moved=2 * 4 * total * feat,
            vmem=20,
        )

    w2a, w2b = shift(w3[:hr], x=1), shift(w1[hr:], x=-1)
    w013 = stack(w0, w1, w3)
    v013 = shift(w013, core=1)
    mine0, other0 = partial(a_far, key, key_far)
    got0 = shift(other0, core=1)
    val_far, w2a, w2b, v013 = lax.optimization_barrier((val_far, w2a, w2b, v013))
    v2 = shift(stack(w2a, w2b), core=1)
    mine1, other1 = partial(a_far, val, val_far)
    got1 = shift(other1, core=1)
    up0, down0 = first_hop(mine0, after(got0, other1))
    up0r, down0r = shift(up0, x=1), shift(down0, x=-1)
    to_up0, to_down0 = second_hop(mine0, got0, up0r, after(down0r, other1))
    from_down0, from_up0 = shift(to_up0, x=1), shift(to_down0, x=-1)
    up1, down1 = first_hop(mine1, after(got1, to_up0))
    up1r, down1r = shift(up1, x=1), shift(down1, x=-1)

    near, out_far = call(
        input_kernel,
        [shape((tok, width)), shape((tok, width // 2))],
        place,
        (after(w013, up1), w2a, w2b, v013, v2, key, val, key_far, val_far),
        [ANY] * 9,
        [ANY] * 2,
        [
            pltpu.VMEM((2, width // 2, feat), BF16),
            pltpu.VMEM((2, 2 * tok, feat), BF16),
            pltpu.VMEM((2 * tok, width // 2), BF16),
            pltpu.SemaphoreType.DMA((22,)),
            pltpu.SemaphoreType.DMA((12,)),
        ],
        flops=4 * tok * width * feat,
        moved=16 * 2**20,
        weight=WEIGHT,
        vmem=20,
    )
    far = shift(out_far, yhi=1)
    to_up1, to_down1 = second_hop(mine1, got1, up1r, after(down1r, out_far))
    from_down1, from_up1 = shift(to_up1, x=1), shift(to_down1, x=-1)
    from_up0 = after(from_up0, to_up1)
    input_grad = call(
        far_columns_kernel,
        shape((tok, width)),
        place,
        (far, near),
        [pl.BlockSpec((tok // 2, width // 2), lambda i, place: (i, 0)), ANY],
        pl.BlockSpec((tok // 2, width // 2), lambda i, place: (i, 1 - place[0])),
        grid=(2,),
        moved=2 * tok * width,
        alias={2: 0},
    )

    half_own = pl.BlockSpec((1, hr, feat), lambda i, place: (place[2], i, 0))
    qc = feat // 4
    half_quarter = pl.BlockSpec((hr, qc), lambda i, place: (i, 0))
    sums0 = (mine0, got0, from_down0, from_up0)
    sum_specs = [half_own, half_own, half_rows, half_rows]
    own, s1, s2, s3 = call(
        selected_kernel,
        [shape((rows, qc), F32)] + [shape((rows, qc))] * 3,
        place,
        (*planes, *sums0),
        [half_rows] * 3 + sum_specs,
        [half_quarter] * 4,
        [pltpu.VMEM((hr, feat), F32)],
        grid=(2,),
        moved=10 * 2**20,
        weight=WEIGHT,
    )
    total = own
    for s, part in ((1, s1), (2, s2), (-1, s3)):
        total = total + shift(part, z=s).astype(F32)
    total, from_down1, from_up1 = lax.optimization_barrier((total, from_down1, from_up1))
    total = lax.reduce_precision(total, 8, 7)
    total = total + after(shift(total.astype(BF16), ylo=1), input_grad).astype(F32)
    mean = (total / 8).astype(BF16)
    means = (mean, shift(mean, z=-1), shift(mean, z=2), shift(mean, z=1))
    sums1 = (mine1, got1, from_down1, from_up1)
    first_out, second_out, inner = call(
        moments_kernel,
        [shape((rows, 2, feat), F32)] * 2 + [shape((rows, feat), F32)],
        place,
        (weight_here, first_moment[0], second_moment[0], *sums0, *sums1),
        [half_both] * 3 + sum_specs * 2,
        [half_both] * 2 + [half_rows],
        grid=(2,),
        moved=16 * 2**20,
    )
    weights_out, anchor_out, momentum_out = call(
        outer_kernel,
        [shape((rows, 2, feat), F32)] + [shape((rows, feat), F32)] * 2,
        place,
        (*means, anchor, momentum, inner),
        [half_quarter] * 4 + [half_rows] * 3,
        [half_both] + [half_rows] * 2,
        [pltpu.VMEM((hr, feat), F32)],
        grid=(2,),
        moved=9 * 2**20,
    )

    return (
        weights_out[None],
        first_out[None],
        second_out[None],
        anchor_out,
        momentum_out,
        input_grad[None],
    )


def solution(mesh):
    fine = Mesh(mesh.devices.reshape(SIZES), AXES)
    rep, fs = ("ylo", "z"), ("yhi", "x", "core")
    in_specs = (
        P(rep, fs, None),
        P(rep, fs, None, None),
        P(rep, fs, None, None),
        P(rep, fs, None, None),
        P(rep, fs, None, None),
        P(fs, None),
        P(fs, None),
    )
    out_specs = (
        P(rep, fs, None, None),
        P(rep, fs, None, None),
        P(rep, fs, None, None),
        P(fs, None),
        P(fs, None),
        P(rep, fs, None),
    )
    return jax.shard_map(shards, mesh=fine, in_specs=in_specs, out_specs=out_specs, check_vma=False)
```

```python
import jax
import jax.numpy as jnp
import numpy as np
from jax import lax
from jax.experimental import pallas as pl
from jax.experimental.pallas import tpu as pltpu
from jax.sharding import Mesh
from jax.sharding import PartitionSpec as P

CORRECT_FIRST = 1.0 - 0.9**8
CORRECT_SECOND = 1.0 - 0.95**8
AXES = ("ylo", "z", "yhi", "x", "core")
SIZES = (2, 4, 2, 4, 2)
BF16 = jnp.bfloat16
F32 = jnp.float32
ANY = pl.BlockSpec(memory_space=pl.ANY)
HBM = pl.BlockSpec(memory_space=pltpu.HBM)
WEIGHT = 50


def shift(value, **steps):
    pairs = []
    for source in np.ndindex(*SIZES):
        target = [(s + steps.get(a, 0)) % n for s, a, n in zip(source, AXES, SIZES)]
        pairs.append(
            (int(np.ravel_multi_index(source, SIZES)), int(np.ravel_multi_index(target, SIZES)))
        )
    return lax.ppermute(value, AXES, pairs)


def call(
    kernel, out_shape, place, inputs, in_specs, out_specs, scratch=(), grid=(1,), flops=0, moved=0, weight=0, alias=None, vmem=12
):
    return pl.pallas_call(
        kernel,
        out_shape=out_shape,
        grid_spec=pltpu.PrefetchScalarGridSpec(
            num_scalar_prefetch=1,
            grid=grid,
            in_specs=in_specs,
            out_specs=out_specs,
            scratch_shapes=list(scratch),
        ),
        compiler_params=pltpu.CompilerParams(vmem_limit_bytes=vmem * 2**20),
        input_output_aliases=alias or {},
        cost_estimate=pl.CostEstimate(flops=weight * 10**9, bytes_accessed=weight * 10**7, transcendentals=0),
    )(place, *inputs)


def after(value, *others):
    return lax.optimization_barrier((value, *others))[0]


def shape(dims, dtype=BF16):
    return jax.ShapeDtypeStruct(dims, dtype)


def far_half_kernel(place, acts, out, sem):
    n = out.shape[1]
    copy = pltpu.make_async_copy(
        acts.at[:, pl.ds(pl.multiple_of((1 - place[0]) * n, 128), n)], out, sem
    )
    copy.start()
    copy.wait()


def stack_kernel(place, *refs):
    out = refs[-1]
    n = 0
    for ref in refs[:-1]:
        out[n : n + ref.shape[0]] = ref[...]
        n += ref.shape[0]


def join_kernel(place, own, far, both):
    n = own.shape[0]
    both[:n] = own[...]
    both[n:] = far[...]


def gradient_kernel(place, a_both, c_own, c_far, mine, other, a_s, c_s, g_s, in_sem, out_sem):
    c = place[1]
    tok, wide = c_own.shape[0], a_both.shape[1]
    rows = mine.shape[1]
    copies = [
        pltpu.make_async_copy(a_both, a_s, in_sem.at[0]),
        pltpu.make_async_copy(c_own, c_s.at[pl.ds(0, tok)], in_sem.at[1]),
        pltpu.make_async_copy(c_far, c_s.at[pl.ds(tok, tok)], in_sem.at[2]),
    ]
    for copy in copies:
        copy.start()
    for copy in copies:
        copy.wait()
    tile = 256
    sends = []
    for i in range(wide // tile):
        cols = slice(i * tile, (i + 1) * tile)
        g_s[cols, :] = lax.dot_general(
            a_s[:, cols], c_s[...], (((0,), (0,)), ((), ())), preferred_element_type=F32
        ).astype(BF16)
        ready = {4: (0, 1), 8: (2, 3)}.get(i, ())
        for core, out in ((1 - c, other), (c, mine)):
            for to in ready:
                start = pl.multiple_of((2 * to + core) * rows, 16)
                sends.append(
                    pltpu.make_async_copy(
                        g_s.at[pl.ds(start, rows)], out.at[to], out_sem.at[len(sends)]
                    )
                )
                sends[-1].start()
    for send in sends:
        send.wait()


def rounded_kernel(place, w, w_low):
    n = w.shape[2]
    w_low[:, :n] = w[:, 0, :].astype(BF16)
    w_low[:, n:] = w[:, 1, :].astype(BF16)


def planes_kernel(place, w, m, v, *planes):
    for f in range(2):
        for whole, plane in zip((w, m, v), planes[3 * f : 3 * f + 3]):
            plane[...] = whole[:, f, :]


def block_sum(mine, got):
    return mine[0].astype(F32) + got[0].astype(F32)


def first_hop_kernel(place, mine, got, up, down):
    part = block_sum(mine, got).astype(BF16)
    n = up.shape[0]
    up[...] = part[:n]
    down[...] = part[n:]


def second_hop_kernel(place, mine_up, got_up, mine_down, got_down, up, down, to_up, to_down):
    n = up.shape[0]
    part = block_sum(mine_up, got_up)
    to_up[:n] = (part[:n] + up[...].astype(F32)).astype(BF16)
    to_up[n:] = part[n:].astype(BF16)
    part = block_sum(mine_down, got_down)
    to_down[:n] = part[:n].astype(BF16)
    to_down[n:] = (part[n:] + down[...].astype(F32)).astype(BF16)


def blocks_kernel(place, *refs):
    for n, out in enumerate(refs[6:]):
        out[...] = block_sum(refs[2 * n], refs[2 * n + 1]).astype(BF16)


def owned_sum(mine, got, *others):
    total = block_sum(mine, got)
    for other in others:
        total = total + other[...].astype(F32)
    return total


def adamw(w, m, v, g):
    m = 0.9 * m + 0.1 * g
    v = 0.95 * v + 0.05 * g * g
    step_dir = m / CORRECT_FIRST / (jnp.sqrt(v / CORRECT_SECOND) + 1e-08)
    return m, v, w - 0.01 * (step_dir + 0.1 * w)


def selected_kernel(place, w, m, v, mine, got, r1, r2, own, s1, s2, s3, m_new, v_new, sel):
    g = owned_sum(mine, got, r1, r2)
    m_new[...], v_new[...], sel[...] = adamw(w[...], m[...], v[...], g)
    n = own.shape[1]
    for step, out in ((0, own), (1, s1), (2, s2), (3, s3)):
        start = pl.multiple_of(lax.rem(place[3] + step, 4) * n, 128)
        out[...] = sel[:, pl.ds(start, n)].astype(out.dtype)


def moments_kernel(place, m_key, v_key, w, m, v, mine, got, r1, r2, r3, first, second, inner):
    g = owned_sum(mine, got, r1, r2, r3)
    m_new, v_new, inner[...] = adamw(w[...], m[...], v[...], g)
    first[:, 0, :] = m_key[...]
    first[:, 1, :] = m_new
    second[:, 0, :] = v_key[...]
    second[:, 1, :] = v_new


def outer_kernel(place, m0, m1, m2, m3, anchor, momentum, inner, weights, anchor_new, momentum_new, mean):
    n = m0.shape[1]
    for step, part in enumerate((m0, m1, m2, m3)):
        start = pl.multiple_of(lax.rem(place[3] + step, 4) * n, 128)
        mean[:, pl.ds(start, n)] = part[...].astype(F32)
    delta = anchor[...] - mean[...]
    moved = 0.9 * momentum[...] + delta
    synced = anchor[...] - 0.7 * (delta + 0.9 * moved)
    momentum_new[...] = moved
    anchor_new[...] = synced
    weights[:, 0, :] = synced
    weights[:, 1, :] = inner[...]


def far_columns_kernel(place, far, near, out):
    out[...] = far[...]


def input_kernel(place, w013, w2, v013, v2, key, val, out, w_s, o_s, sem, out_sem):
    h, c, x = place[0], place[1], place[2]
    rows, feat = v2.shape[0], key.shape[1]
    wide = o_s.shape[1]
    pieces = []
    for core, triple, last in ((c, w013, w2), (1 - c, v013, v2)):
        for n, step in enumerate((0, 1, 3)):
            pieces.append((core, step, triple, n * rows))
        pieces.append((core, 2, last, 0))
    copies = [[], []]
    for f in range(2):
        for core, step, piece, first in pieces:
            start = pl.multiple_of((2 * lax.rem(x + step, 4) + core) * rows, 16)
            copies[f].append(
                pltpu.make_async_copy(
                    piece.at[pl.ds(first, rows), pl.ds(f * feat, feat)],
                    w_s.at[f, pl.ds(start, rows)],
                    sem.at[8 * f + len(copies[f])],
                )
            )
    for copy in copies[0] + copies[1]:
        copy.start()
    tile = 384
    tiles = [slice(j * tile, (j + 1) * tile) for j in range(wide // tile)]
    dims = (((1,), (1,)), ((), ()))
    for copy in copies[0]:
        copy.wait()
    accs = [
        lax.dot_general(key[...], w_s[0, cols, :], dims, preferred_element_type=F32)
        for cols in tiles
    ]
    for copy in copies[1]:
        copy.wait()
    base = h * wide if out.shape[1] > wide else 0
    sends = []
    for j, cols in enumerate(tiles):
        acc = lax.dot_general(val[...], w_s[1, cols, :], dims, preferred_element_type=F32)
        o_s[:, cols] = (accs[j] + acc).astype(BF16)
        sends.append(
            pltpu.make_async_copy(
                o_s.at[:, pl.ds(j * tile, tile)],
                out.at[:, pl.ds(pl.multiple_of(base + j * tile, 128), tile)],
                out_sem.at[j],
            )
        )
        sends[-1].start()
    for send in sends:
        send.wait()


def shards(activations, cotangent, weights, first_moment, second_moment, anchor, momentum):
    acts = activations[0]
    tok, width = acts.shape
    weight_here = weights[0]
    rows = weight_here.shape[0]
    feat = weight_here.shape[2]
    ylo, z, h, x, c = [lax.axis_index(a) for a in AXES]
    place = jnp.stack([h, c, x, z]).astype(jnp.int32)
    hr = rows // 2

    def whole(*dims):
        return pl.BlockSpec(dims, lambda i, place: (0,) * len(dims))

    half_rows = pl.BlockSpec((hr, feat), lambda i, place: (i, 0))
    half_both = pl.BlockSpec((hr, 2, feat), lambda i, place: (i, 0, 0))
    a_send = call(
        far_half_kernel,
        shape((tok, width // 2)),
        place,
        (acts,),
        [ANY],
        ANY,
        [pltpu.SemaphoreType.DMA],
        moved=2 * tok * width,
    )
    w0 = call(
        rounded_kernel,
        shape((rows, 2 * feat)),
        place,
        (after(weight_here, a_send),),
        [half_both],
        pl.BlockSpec((hr, 2 * feat), lambda i, place: (i, 0)),
        grid=(2,),
        moved=5 * 2**20,
        weight=WEIGHT,
    )
    w1, w3 = shift(w0, x=-1), shift(w0, x=1)
    a_far = shift(a_send, yhi=1)
    cot = after(cotangent, w0, a_send)[0]
    key, val = cot[:, 0, :], cot[:, 1, :]
    key_far = shift(key, yhi=1)

    planes = call(
        planes_kernel,
        [shape((rows, feat), F32)] * 6,
        place,
        (after(weight_here, key), first_moment[0], second_moment[0]),
        [half_both] * 3,
        [half_rows] * 6,
        grid=(2,),
        moved=14 * 2**20,
        vmem=20,
    )
    val_far = shift(after(val, planes[0]), yhi=1)

    def partial(a, c_own, c_far):
        return call(
            gradient_kernel,
            [shape((4, rows, feat))] * 2,
            place,
            (a, c_own, c_far),
            [ANY] * 3,
            [ANY] * 2,
            [
                pltpu.VMEM((2 * tok, width // 2), BF16),
                pltpu.VMEM((2 * tok, feat), BF16),
                pltpu.VMEM((width // 2, feat), BF16),
                pltpu.SemaphoreType.DMA((3,)),
                pltpu.SemaphoreType.DMA((8,)),
            ],
            flops=2 * tok * width * feat,
            moved=12 * 2**20,
            weight=WEIGHT,
            vmem=16,
        )

    def block(step):
        return pl.BlockSpec((1, rows, feat), lambda i, place: (lax.rem(place[2] + step, 4), 0, 0))

    def first_hop(mine, got):
        up, down = call(
            first_hop_kernel,
            [shape((hr, feat))] * 2,
            place,
            (mine, got),
            [block(2)] * 2,
            [whole(hr, feat)] * 2,
            moved=2**21,
        )
        return up, down

    def second_hop(mine, got, up, down, weight=0):
        return call(
            second_hop_kernel,
            [shape((rows, feat))] * 2,
            place,
            (mine, got, mine, got, up, down),
            [block(1), block(1), block(3), block(3), whole(hr, feat), whole(hr, feat)],
            [whole(rows, feat)] * 2,
            moved=2**22,
            weight=weight,
        )

    def blocks(mine, got):
        return call(
            blocks_kernel,
            [shape((rows, feat))] * 3,
            place,
            (mine, got) * 3,
            [block(1), block(1), block(2), block(2), block(3), block(3)],
            [whole(rows, feat)] * 3,
            moved=2**22,
        )

    a_both = call(
        join_kernel,
        shape((2 * tok, width // 2)),
        place,
        (acts, after(a_far, planes[0])),
        [
            pl.BlockSpec((tok, width // 2), lambda i, place: (0, place[0])),
            whole(tok, width // 2),
        ],
        whole(2 * tok, width // 2),
        moved=5 * 2**20,
        weight=WEIGHT,
        vmem=16,
    )
    a_both, w1, w3, planes = lax.optimization_barrier((a_both, w1, w3, planes))
    def stack(*parts, weight=0):
        total = sum(p.shape[0] for p in parts)
        return call(
            stack_kernel,
            shape((total, 2 * feat)),
            place,
            parts,
            [whole(*p.shape) for p in parts],
            whole(total, 2 * feat),
            moved=2 * 4 * total * feat,
            weight=weight,
            vmem=20,
        )

    w2a, w2b = shift(w3[:hr], x=1), shift(w1[hr:], x=-1)
    w013 = stack(w0, w1, w3)
    v013 = shift(w013, core=1)
    mine0, other0 = partial(a_both, key, key_far)
    got0 = shift(other0, core=1)
    val_far, w2a, w2b, v013 = lax.optimization_barrier((val_far, w2a, w2b, v013))
    w2 = stack(w2a, w2b, weight=WEIGHT)
    v2 = shift(w2, core=1)
    up0, down0 = first_hop(mine0, after(got0, w2))
    up0r, down0r = shift(up0, x=1), shift(down0, x=-1)
    mine1, other1 = partial(a_both, val, after(val_far, up0))
    got1 = shift(other1, core=1)
    to_up0, to_down0 = second_hop(mine0, got0, up0r, after(down0r, other1))
    key_parts = (shift(to_up0, x=1), shift(to_down0, x=-1))

    def input_part(first, key, val, columns, weight=0):
        return call(
            input_kernel,
            shape((tok, columns)),
            place,
            (first, w2, v013, v2, key, val),
            [ANY] * 4 + [whole(tok, feat)] * 2,
            ANY,
            [
                pltpu.VMEM((2, width // 2, feat), BF16),
                pltpu.VMEM((tok, width // 2), BF16),
                pltpu.SemaphoreType.DMA((16,)),
                pltpu.SemaphoreType.DMA((6,)),
            ],
            flops=2 * tok * width * feat,
            moved=12 * 2**20,
            weight=weight,
            vmem=20,
        )

    out_far = input_part(after(w013, to_up0), key_far, val_far, width // 2, WEIGHT)
    far = shift(out_far, yhi=1)
    u1, u2, u3 = blocks(mine1, after(got1, out_far))
    val_parts = (shift(u1, x=1), shift(u3, x=-1))
    key_parts = after(key_parts, u1)

    half_own = pl.BlockSpec((1, hr, feat), lambda i, place: (place[2], i, 0))
    qc = feat // 4
    half_quarter = pl.BlockSpec((hr, qc), lambda i, place: (i, 0))
    sums0 = (mine0, got0, *key_parts)
    sum_specs = [half_own] * 2 + [half_rows] * 2
    own, s1, s2, s3, m_key, v_key = call(
        selected_kernel,
        [shape((rows, qc), F32)] + [shape((rows, qc))] * 3 + [shape((rows, feat), F32)] * 2,
        place,
        (*planes[:3], *sums0),
        [half_rows] * 3 + sum_specs,
        [half_quarter] * 4 + [half_rows] * 2,
        [pltpu.VMEM((hr, feat), F32)],
        grid=(2,),
        moved=10 * 2**20,
        weight=WEIGHT,
    )
    parts = [shift(part, z=step) for step, part in ((1, s1), (2, s2), (-1, s3))]
    val_parts = (*val_parts, shift(after(u2, *parts), x=2))
    total = own
    for part in parts:
        total = total + part.astype(F32)
    near = input_part(after(w013, total), key, val, width)
    input_grad = call(
        far_columns_kernel,
        shape((tok, width)),
        place,
        (far, near),
        [pl.BlockSpec((tok // 2, width // 2), lambda i, place: (i, 0)), ANY],
        pl.BlockSpec((tok // 2, width // 2), lambda i, place: (i, 1 - place[0])),
        grid=(2,),
        moved=2 * tok * width,
        alias={2: 0},
    )

    total, r1, r3 = lax.optimization_barrier((total, *val_parts[:2]))
    val_parts = (r1, r3, val_parts[2])
    total = lax.reduce_precision(total, 8, 7)
    total = total + after(shift(total.astype(BF16), ylo=1), input_grad).astype(F32)
    mean = (total / 8).astype(BF16)
    means = (mean, shift(mean, z=-1), shift(mean, z=2), shift(mean, z=1))
    sums1 = (mine1, got1, *val_parts)
    first_out, second_out, inner = call(
        moments_kernel,
        [shape((rows, 2, feat), F32)] * 2 + [shape((rows, feat), F32)],
        place,
        (m_key, v_key, *planes[3:], *sums1),
        [half_rows] * 5 + sum_specs + [half_rows],
        [half_both] * 2 + [half_rows],
        grid=(2,),
        moved=16 * 2**20,
    )
    weights_out, anchor_out, momentum_out = call(
        outer_kernel,
        [shape((rows, 2, feat), F32)] + [shape((rows, feat), F32)] * 2,
        place,
        (*means, anchor, momentum, inner),
        [half_quarter] * 4 + [half_rows] * 3,
        [half_both] + [half_rows] * 2,
        [pltpu.VMEM((hr, feat), F32)],
        grid=(2,),
        moved=9 * 2**20,
    )

    return (
        weights_out[None],
        first_out[None],
        second_out[None],
        anchor_out,
        momentum_out,
        input_grad[None],
    )


def solution(mesh):
    fine = Mesh(mesh.devices.reshape(SIZES), AXES)
    rep, fs = ("ylo", "z"), ("yhi", "x", "core")
    in_specs = (
        P(rep, fs, None),
        P(rep, fs, None, None),
        P(rep, fs, None, None),
        P(rep, fs, None, None),
        P(rep, fs, None, None),
        P(fs, None),
        P(fs, None),
    )
    out_specs = (
        P(rep, fs, None, None),
        P(rep, fs, None, None),
        P(rep, fs, None, None),
        P(fs, None),
        P(fs, None),
        P(rep, fs, None),
    )
    return jax.shard_map(shards, mesh=fine, in_specs=in_specs, out_specs=out_specs, check_vma=False)
```

```python
import jax
import jax.numpy as jnp
import numpy as np
from jax import lax
from jax.experimental import pallas as pl
from jax.experimental.pallas import tpu as pltpu
from jax.sharding import Mesh
from jax.sharding import PartitionSpec as P

CORRECT_FIRST = 1.0 - 0.9**8
CORRECT_SECOND = 1.0 - 0.95**8
AXES = ("ylo", "z", "yhi", "x", "core")
SIZES = (2, 4, 2, 4, 2)
BF16 = jnp.bfloat16
F32 = jnp.float32
ANY = pl.BlockSpec(memory_space=pl.ANY)
HBM = pl.BlockSpec(memory_space=pltpu.HBM)
WEIGHT = 50


def shift(value, **steps):
    pairs = []
    for source in np.ndindex(*SIZES):
        target = [(s + steps.get(a, 0)) % n for s, a, n in zip(source, AXES, SIZES)]
        pairs.append(
            (int(np.ravel_multi_index(source, SIZES)), int(np.ravel_multi_index(target, SIZES)))
        )
    return lax.ppermute(value, AXES, pairs)


def call(
    kernel, out_shape, place, inputs, in_specs, out_specs, scratch=(), grid=(1,), flops=0, moved=0, weight=0, alias=None, vmem=12
):
    return pl.pallas_call(
        kernel,
        out_shape=out_shape,
        grid_spec=pltpu.PrefetchScalarGridSpec(
            num_scalar_prefetch=1,
            grid=grid,
            in_specs=in_specs,
            out_specs=out_specs,
            scratch_shapes=list(scratch),
        ),
        compiler_params=pltpu.CompilerParams(vmem_limit_bytes=vmem * 2**20),
        input_output_aliases=alias or {},
        cost_estimate=pl.CostEstimate(flops=weight * 10**9, bytes_accessed=weight * 10**7, transcendentals=0),
    )(place, *inputs)


def after(value, *others):
    return lax.optimization_barrier((value, *others))[0]


def shape(dims, dtype=BF16):
    return jax.ShapeDtypeStruct(dims, dtype)


def far_half_kernel(place, acts, out, sem):
    n = out.shape[1]
    copy = pltpu.make_async_copy(
        acts.at[:, pl.ds(pl.multiple_of((1 - place[0]) * n, 128), n)], out, sem
    )
    copy.start()
    copy.wait()


def stack_kernel(place, *refs):
    out = refs[-1]
    n = 0
    for ref in refs[:-1]:
        out[n : n + ref.shape[0]] = ref[...]
        n += ref.shape[0]


def join_kernel(place, own, far, both):
    n = own.shape[0]
    both[:n] = own[...]
    both[n:] = far[...]


def gradient_kernel(place, a_both, c_own, c_far, mine, other, a_s, c_s, g_s, in_sem, out_sem):
    c = place[1]
    tok, wide = c_own.shape[0], a_both.shape[1]
    rows = mine.shape[1]
    copies = [
        pltpu.make_async_copy(a_both, a_s, in_sem.at[0]),
        pltpu.make_async_copy(c_own, c_s.at[pl.ds(0, tok)], in_sem.at[1]),
        pltpu.make_async_copy(c_far, c_s.at[pl.ds(tok, tok)], in_sem.at[2]),
    ]
    for copy in copies:
        copy.start()
    for copy in copies:
        copy.wait()
    tile = 256
    sends = []
    for i in range(wide // tile):
        cols = slice(i * tile, (i + 1) * tile)
        g_s[cols, :] = lax.dot_general(
            a_s[:, cols], c_s[...], (((0,), (0,)), ((), ())), preferred_element_type=F32
        ).astype(BF16)
        ready = {4: (0, 1), 8: (2, 3)}.get(i, ())
        for core, out in ((1 - c, other), (c, mine)):
            for to in ready:
                start = pl.multiple_of((2 * to + core) * rows, 16)
                sends.append(
                    pltpu.make_async_copy(
                        g_s.at[pl.ds(start, rows)], out.at[to], out_sem.at[len(sends)]
                    )
                )
                sends[-1].start()
    for send in sends:
        send.wait()


def rounded_kernel(place, w, w_low):
    n = w.shape[2]
    w_low[:, :n] = w[:, 0, :].astype(BF16)
    w_low[:, n:] = w[:, 1, :].astype(BF16)


def planes_kernel(place, w, m, v, *planes):
    for f in range(2):
        for whole, plane in zip((w, m, v), planes[3 * f : 3 * f + 3]):
            plane[...] = whole[:, f, :]


def block_sum(mine, got):
    return mine[0].astype(F32) + got[0].astype(F32)


def first_hop_kernel(place, mine, got, up, down):
    part = block_sum(mine, got).astype(BF16)
    n = up.shape[0]
    up[...] = part[:n]
    down[...] = part[n:]


def second_hop_kernel(place, mine_up, got_up, mine_down, got_down, up, down, to_up, to_down):
    n = up.shape[0]
    part = block_sum(mine_up, got_up)
    to_up[:n] = (part[:n] + up[...].astype(F32)).astype(BF16)
    to_up[n:] = part[n:].astype(BF16)
    part = block_sum(mine_down, got_down)
    to_down[:n] = part[:n].astype(BF16)
    to_down[n:] = (part[n:] + down[...].astype(F32)).astype(BF16)


def owned_sum(mine, got, *others):
    total = block_sum(mine, got)
    for other in others:
        total = total + other[...].astype(F32)
    return total


def adamw(w, m, v, g):
    m = 0.9 * m + 0.1 * g
    v = 0.95 * v + 0.05 * g * g
    step_dir = m / CORRECT_FIRST / (jnp.sqrt(v / CORRECT_SECOND) + 1e-08)
    return m, v, w - 0.01 * (step_dir + 0.1 * w)


def selected_kernel(place, w, m, v, mine, got, r1, r2, own, s1, s2, s3, m_new, v_new, sel):
    g = owned_sum(mine, got, r1, r2)
    m_new[...], v_new[...], sel[...] = adamw(w[...], m[...], v[...], g)
    n = own.shape[1]
    for step, out in ((0, own), (1, s1), (2, s2), (3, s3)):
        start = pl.multiple_of(lax.rem(place[3] + step, 4) * n, 128)
        out[...] = sel[:, pl.ds(start, n)].astype(out.dtype)


def moments_kernel(place, m_key, v_key, w, m, v, mine, got, r1, r2, first, second, inner):
    g = owned_sum(mine, got, r1, r2)
    m_new, v_new, inner[...] = adamw(w[...], m[...], v[...], g)
    first[:, 0, :] = m_key[...]
    first[:, 1, :] = m_new
    second[:, 0, :] = v_key[...]
    second[:, 1, :] = v_new


def outer_kernel(place, m0, m1, m2, m3, anchor, momentum, inner, weights, anchor_new, momentum_new, mean):
    n = m0.shape[1]
    for step, part in enumerate((m0, m1, m2, m3)):
        start = pl.multiple_of(lax.rem(place[3] + step, 4) * n, 128)
        mean[:, pl.ds(start, n)] = part[...].astype(F32)
    delta = anchor[...] - mean[...]
    moved = 0.9 * momentum[...] + delta
    synced = anchor[...] - 0.7 * (delta + 0.9 * moved)
    momentum_new[...] = moved
    anchor_new[...] = synced
    weights[:, 0, :] = synced
    weights[:, 1, :] = inner[...]


def far_columns_kernel(place, far, near, out):
    out[...] = far[...]


def input_kernel(place, w013, w2, v013, v2, key, val, out, w_s, o_s, sem, out_sem):
    h, c, x = place[0], place[1], place[2]
    rows, feat = v2.shape[0], key.shape[1]
    wide = o_s.shape[1]
    pieces = []
    for core, triple, last in ((c, w013, w2), (1 - c, v013, v2)):
        for n, step in enumerate((0, 1, 3)):
            pieces.append((core, step, triple, n * rows))
        pieces.append((core, 2, last, 0))
    copies = [[], []]
    for f in range(2):
        for core, step, piece, first in pieces:
            start = pl.multiple_of((2 * lax.rem(x + step, 4) + core) * rows, 16)
            copies[f].append(
                pltpu.make_async_copy(
                    piece.at[pl.ds(first, rows), pl.ds(f * feat, feat)],
                    w_s.at[f, pl.ds(start, rows)],
                    sem.at[8 * f + len(copies[f])],
                )
            )
    for copy in copies[0] + copies[1]:
        copy.start()
    tile = 384
    tiles = [slice(j * tile, (j + 1) * tile) for j in range(wide // tile)]
    dims = (((1,), (1,)), ((), ()))
    for copy in copies[0]:
        copy.wait()
    accs = [
        lax.dot_general(key[...], w_s[0, cols, :], dims, preferred_element_type=F32)
        for cols in tiles
    ]
    for copy in copies[1]:
        copy.wait()
    base = h * wide if out.shape[1] > wide else 0
    sends = []
    for j, cols in enumerate(tiles):
        acc = lax.dot_general(val[...], w_s[1, cols, :], dims, preferred_element_type=F32)
        o_s[:, cols] = (accs[j] + acc).astype(BF16)
        sends.append(
            pltpu.make_async_copy(
                o_s.at[:, pl.ds(j * tile, tile)],
                out.at[:, pl.ds(pl.multiple_of(base + j * tile, 128), tile)],
                out_sem.at[j],
            )
        )
        sends[-1].start()
    for send in sends:
        send.wait()


def shards(activations, cotangent, weights, first_moment, second_moment, anchor, momentum):
    acts = activations[0]
    tok, width = acts.shape
    weight_here = weights[0]
    rows = weight_here.shape[0]
    feat = weight_here.shape[2]
    ylo, z, h, x, c = [lax.axis_index(a) for a in AXES]
    place = jnp.stack([h, c, x, z]).astype(jnp.int32)
    hr = rows // 2

    def whole(*dims):
        return pl.BlockSpec(dims, lambda i, place: (0,) * len(dims))

    half_rows = pl.BlockSpec((hr, feat), lambda i, place: (i, 0))
    half_both = pl.BlockSpec((hr, 2, feat), lambda i, place: (i, 0, 0))
    a_send = call(
        far_half_kernel,
        shape((tok, width // 2)),
        place,
        (acts,),
        [ANY],
        ANY,
        [pltpu.SemaphoreType.DMA],
        moved=2 * tok * width,
    )
    w0 = call(
        rounded_kernel,
        shape((rows, 2 * feat)),
        place,
        (after(weight_here, a_send),),
        [half_both],
        pl.BlockSpec((hr, 2 * feat), lambda i, place: (i, 0)),
        grid=(2,),
        moved=5 * 2**20,
        weight=WEIGHT,
    )
    w1, w3 = shift(w0, x=-1), shift(w0, x=1)
    a_far = shift(a_send, yhi=1)
    cot = after(cotangent, w0, a_send)[0]
    key, val = cot[:, 0, :], cot[:, 1, :]
    key_far = shift(key, yhi=1)

    planes = call(
        planes_kernel,
        [shape((rows, feat), F32)] * 6,
        place,
        (after(weight_here, key), first_moment[0], second_moment[0]),
        [half_both] * 3,
        [half_rows] * 6,
        grid=(2,),
        moved=14 * 2**20,
        vmem=20,
    )
    val_far = shift(after(val, planes[0]), yhi=1)

    def partial(a, c_own, c_far):
        return call(
            gradient_kernel,
            [shape((4, rows, feat))] * 2,
            place,
            (a, c_own, c_far),
            [ANY] * 3,
            [ANY] * 2,
            [
                pltpu.VMEM((2 * tok, width // 2), BF16),
                pltpu.VMEM((2 * tok, feat), BF16),
                pltpu.VMEM((width // 2, feat), BF16),
                pltpu.SemaphoreType.DMA((3,)),
                pltpu.SemaphoreType.DMA((8,)),
            ],
            flops=2 * tok * width * feat,
            moved=12 * 2**20,
            weight=WEIGHT,
            vmem=16,
        )

    def block(step):
        return pl.BlockSpec((1, rows, feat), lambda i, place: (lax.rem(place[2] + step, 4), 0, 0))

    def first_hop(mine, got):
        up, down = call(
            first_hop_kernel,
            [shape((hr, feat))] * 2,
            place,
            (mine, got),
            [block(2)] * 2,
            [whole(hr, feat)] * 2,
            moved=2**21,
        )
        return up, down

    def second_hop(mine, got, up, down, weight=0):
        return call(
            second_hop_kernel,
            [shape((rows, feat))] * 2,
            place,
            (mine, got, mine, got, up, down),
            [block(1), block(1), block(3), block(3), whole(hr, feat), whole(hr, feat)],
            [whole(rows, feat)] * 2,
            moved=2**22,
            weight=weight,
        )

    a_both = call(
        join_kernel,
        shape((2 * tok, width // 2)),
        place,
        (acts, after(a_far, planes[0])),
        [
            pl.BlockSpec((tok, width // 2), lambda i, place: (0, place[0])),
            whole(tok, width // 2),
        ],
        whole(2 * tok, width // 2),
        moved=5 * 2**20,
        weight=WEIGHT,
        vmem=16,
    )
    a_both, w1, w3, planes = lax.optimization_barrier((a_both, w1, w3, planes))
    def stack(*parts, weight=0):
        total = sum(p.shape[0] for p in parts)
        return call(
            stack_kernel,
            shape((total, 2 * feat)),
            place,
            parts,
            [whole(*p.shape) for p in parts],
            whole(total, 2 * feat),
            moved=2 * 4 * total * feat,
            weight=weight,
            vmem=20,
        )

    w2a, w2b = shift(w3[:hr], x=1), shift(w1[hr:], x=-1)
    w013 = stack(w0, w1, w3)
    v013 = shift(w013, core=1)
    mine0, other0 = partial(a_both, key, key_far)
    got0 = shift(other0, core=1)
    val_far, w2a, w2b, v013 = lax.optimization_barrier((val_far, w2a, w2b, v013))
    w2 = stack(w2a, w2b, weight=WEIGHT)
    v2 = shift(w2, core=1)
    up0, down0 = first_hop(mine0, after(got0, w2))
    up0r, down0r = shift(up0, x=1), shift(down0, x=-1)
    mine1, other1 = partial(a_both, val, after(val_far, up0))
    got1 = shift(other1, core=1)
    to_up0, to_down0 = second_hop(mine0, got0, up0r, after(down0r, other1))
    key_parts = (shift(to_up0, x=1), shift(to_down0, x=-1))

    def input_part(first, key, val, columns, weight=0):
        return call(
            input_kernel,
            shape((tok, columns)),
            place,
            (first, w2, v013, v2, key, val),
            [ANY] * 4 + [whole(tok, feat)] * 2,
            ANY,
            [
                pltpu.VMEM((2, width // 2, feat), BF16),
                pltpu.VMEM((tok, width // 2), BF16),
                pltpu.SemaphoreType.DMA((16,)),
                pltpu.SemaphoreType.DMA((6,)),
            ],
            flops=2 * tok * width * feat,
            moved=12 * 2**20,
            weight=weight,
            vmem=20,
        )

    out_far = input_part(after(w013, to_up0), key_far, val_far, width // 2, WEIGHT)
    far = shift(out_far, yhi=1)
    up1, down1 = first_hop(mine1, after(got1, out_far))
    up1r, down1r = shift(up1, x=1), shift(down1, x=-1)
    key_parts = after(key_parts, up1)

    half_own = pl.BlockSpec((1, hr, feat), lambda i, place: (place[2], i, 0))
    qc = feat // 4
    half_quarter = pl.BlockSpec((hr, qc), lambda i, place: (i, 0))
    sums0 = (mine0, got0, *key_parts)
    sum_specs = [half_own] * 2 + [half_rows] * 2
    own, s1, s2, s3, m_key, v_key = call(
        selected_kernel,
        [shape((rows, qc), F32)] + [shape((rows, qc))] * 3 + [shape((rows, feat), F32)] * 2,
        place,
        (*planes[:3], *sums0),
        [half_rows] * 3 + sum_specs,
        [half_quarter] * 4 + [half_rows] * 2,
        [pltpu.VMEM((hr, feat), F32)],
        grid=(2,),
        moved=10 * 2**20,
        weight=WEIGHT,
    )
    to_up1, to_down1 = second_hop(mine1, got1, up1r, after(down1r, own))
    val_parts = (shift(to_up1, x=1), shift(to_down1, x=-1))
    parts = [shift(part, z=step) for step, part in ((1, s1), (2, s2), (-1, s3))]
    total = own
    for part in parts:
        total = total + part.astype(F32)
    near = input_part(after(w013, total), key, val, width)
    input_grad = call(
        far_columns_kernel,
        shape((tok, width)),
        place,
        (far, near),
        [pl.BlockSpec((tok // 2, width // 2), lambda i, place: (i, 0)), ANY],
        pl.BlockSpec((tok // 2, width // 2), lambda i, place: (i, 1 - place[0])),
        grid=(2,),
        moved=2 * tok * width,
        alias={2: 0},
    )

    total = lax.reduce_precision(total, 8, 7)
    total = total + after(shift(total.astype(BF16), ylo=1), input_grad).astype(F32)
    mean = (total / 8).astype(BF16)
    means = (mean, shift(mean, z=-1), shift(mean, z=2), shift(mean, z=1))
    sums1 = (mine1, got1, *val_parts)
    first_out, second_out, inner = call(
        moments_kernel,
        [shape((rows, 2, feat), F32)] * 2 + [shape((rows, feat), F32)],
        place,
        (m_key, v_key, *planes[3:], *sums1),
        [half_rows] * 5 + sum_specs,
        [half_both] * 2 + [half_rows],
        grid=(2,),
        moved=16 * 2**20,
    )
    weights_out, anchor_out, momentum_out = call(
        outer_kernel,
        [shape((rows, 2, feat), F32)] + [shape((rows, feat), F32)] * 2,
        place,
        (*means, anchor, momentum, inner),
        [half_quarter] * 4 + [half_rows] * 3,
        [half_both] + [half_rows] * 2,
        [pltpu.VMEM((hr, feat), F32)],
        grid=(2,),
        moved=9 * 2**20,
    )

    return (
        weights_out[None],
        first_out[None],
        second_out[None],
        anchor_out,
        momentum_out,
        input_grad[None],
    )


def solution(mesh):
    fine = Mesh(mesh.devices.reshape(SIZES), AXES)
    rep, fs = ("ylo", "z"), ("yhi", "x", "core")
    in_specs = (
        P(rep, fs, None),
        P(rep, fs, None, None),
        P(rep, fs, None, None),
        P(rep, fs, None, None),
        P(rep, fs, None, None),
        P(fs, None),
        P(fs, None),
    )
    out_specs = (
        P(rep, fs, None, None),
        P(rep, fs, None, None),
        P(rep, fs, None, None),
        P(fs, None),
        P(fs, None),
        P(rep, fs, None),
    )
    return jax.shard_map(shards, mesh=fine, in_specs=in_specs, out_specs=out_specs, check_vma=False)
```

```python
import functools

import jax
import jax.numpy as jnp
import numpy as np
from jax import lax
from jax.experimental import pallas as pl
from jax.experimental.pallas import tpu as pltpu
from jax.sharding import Mesh
from jax.sharding import PartitionSpec as P

CORRECT_FIRST = 1.0 - 0.9**8
CORRECT_SECOND = 1.0 - 0.95**8
AXES = ("ylo", "z", "yhi", "x", "core")
SIZES = (2, 4, 2, 4, 2)
BF16 = jnp.bfloat16
F32 = jnp.float32
ANY = pl.BlockSpec(memory_space=pl.ANY)
HBM = pl.BlockSpec(memory_space=pltpu.HBM)
WEIGHT = 50


def shift(value, **steps):
    pairs = []
    for source in np.ndindex(*SIZES):
        target = [(s + steps.get(a, 0)) % n for s, a, n in zip(source, AXES, SIZES)]
        pairs.append(
            (int(np.ravel_multi_index(source, SIZES)), int(np.ravel_multi_index(target, SIZES)))
        )
    return lax.ppermute(value, AXES, pairs)


def call(
    kernel, out_shape, place, inputs, in_specs, out_specs, scratch=(), grid=(1,), flops=0, moved=0, weight=0, alias=None, vmem=12
):
    return pl.pallas_call(
        kernel,
        out_shape=out_shape,
        grid_spec=pltpu.PrefetchScalarGridSpec(
            num_scalar_prefetch=1,
            grid=grid,
            in_specs=in_specs,
            out_specs=out_specs,
            scratch_shapes=list(scratch),
        ),
        compiler_params=pltpu.CompilerParams(vmem_limit_bytes=vmem * 2**20),
        input_output_aliases=alias or {},
        cost_estimate=pl.CostEstimate(flops=weight * 10**9, bytes_accessed=weight * 10**7, transcendentals=0),
    )(place, *inputs)


def after(value, *others):
    return lax.optimization_barrier((value, *others))[0]


def shape(dims, dtype=BF16):
    return jax.ShapeDtypeStruct(dims, dtype)


def far_half_kernel(place, acts, out, sem):
    n = out.shape[1]
    copy = pltpu.make_async_copy(
        acts.at[:, pl.ds(pl.multiple_of((1 - place[0]) * n, 128), n)], out, sem
    )
    copy.start()
    copy.wait()


def stack_kernel(place, *refs):
    out = refs[-1]
    n = 0
    for ref in refs[:-1]:
        out[n : n + ref.shape[0]] = ref[...]
        n += ref.shape[0]


def join_kernel(place, own, far, both):
    n = own.shape[0]
    both[:n] = own[...]
    both[n:] = far[...]


def gradient_kernel(place, a_both, c_own, c_far, mine, other, a_s, c_s, g_s, in_sem, out_sem):
    c = place[1]
    tok, wide = c_own.shape[0], a_both.shape[1]
    rows = mine.shape[1]
    copies = [
        pltpu.make_async_copy(a_both, a_s, in_sem.at[0]),
        pltpu.make_async_copy(c_own, c_s.at[pl.ds(0, tok)], in_sem.at[1]),
        pltpu.make_async_copy(c_far, c_s.at[pl.ds(tok, tok)], in_sem.at[2]),
    ]
    for copy in copies:
        copy.start()
    for copy in copies:
        copy.wait()
    tile = 256
    sends = []
    for i in range(wide // tile):
        cols = slice(i * tile, (i + 1) * tile)
        g_s[cols, :] = lax.dot_general(
            a_s[:, cols], c_s[...], (((0,), (0,)), ((), ())), preferred_element_type=F32
        ).astype(BF16)
        ready = {4: (0, 1), 8: (2, 3)}.get(i, ())
        for core, out in ((1 - c, other), (c, mine)):
            for to in ready:
                start = pl.multiple_of((2 * to + core) * rows, 16)
                sends.append(
                    pltpu.make_async_copy(
                        g_s.at[pl.ds(start, rows)], out.at[to], out_sem.at[len(sends)]
                    )
                )
                sends[-1].start()
    for send in sends:
        send.wait()


def rounded_kernel(place, w, w_low):
    n = w.shape[2]
    w_low[:, :n] = w[:, 0, :].astype(BF16)
    w_low[:, n:] = w[:, 1, :].astype(BF16)


def planes_kernel(place, w, m, v, *planes):
    for f in range(2):
        for whole, plane in zip((w, m, v), planes[3 * f : 3 * f + 3]):
            plane[...] = whole[:, f, :]


def block_sum(mine, got):
    return mine[0].astype(F32) + got[0].astype(F32)


def first_hop_kernel(place, mine, got, up, down):
    part = block_sum(mine, got).astype(BF16)
    n = up.shape[0]
    up[...] = part[:n]
    down[...] = part[n:]


def second_hop_kernel(place, mine_up, got_up, mine_down, got_down, up, down, to_up, to_down):
    n = up.shape[0]
    part = block_sum(mine_up, got_up)
    to_up[:n] = (part[:n] + up[...].astype(F32)).astype(BF16)
    to_up[n:] = part[n:].astype(BF16)
    part = block_sum(mine_down, got_down)
    to_down[:n] = part[:n].astype(BF16)
    to_down[n:] = (part[n:] + down[...].astype(F32)).astype(BF16)


def owned_sum(mine, got, *others):
    total = block_sum(mine, got)
    for other in others:
        total = total + other[...].astype(F32)
    return total


def adamw(w, m, v, g):
    m = 0.9 * m + 0.1 * g
    v = 0.95 * v + 0.05 * g * g
    step_dir = m / CORRECT_FIRST / (jnp.sqrt(v / CORRECT_SECOND) + 1e-08)
    return m, v, w - 0.01 * (step_dir + 0.1 * w)


def selected_kernel(place, w, m, v, mine, got, r1, r2, own, s1, s2, s3, m_new, v_new, sel):
    g = owned_sum(mine, got, r1, r2)
    m_new[...], v_new[...], sel[...] = adamw(w[...], m[...], v[...], g)
    n = own.shape[1]
    for step, out in ((0, own), (1, s1), (2, s2), (3, s3)):
        start = pl.multiple_of(lax.rem(place[3] + step, 4) * n, 128)
        out[...] = sel[:, pl.ds(start, n)].astype(out.dtype)


def moments_kernel(place, m_key, v_key, w, m, v, mine, got, r1, r2, first, second, inner):
    g = owned_sum(mine, got, r1, r2)
    m_new, v_new, inner[...] = adamw(w[...], m[...], v[...], g)
    first[:, 0, :] = m_key[...]
    first[:, 1, :] = m_new
    second[:, 0, :] = v_key[...]
    second[:, 1, :] = v_new


def outer_kernel(place, m0, m1, m2, m3, anchor, momentum, inner, weights, anchor_new, momentum_new, mean):
    n = m0.shape[1]
    for step, part in enumerate((m0, m1, m2, m3)):
        start = pl.multiple_of(lax.rem(place[3] + step, 4) * n, 128)
        mean[:, pl.ds(start, n)] = part[...].astype(F32)
    delta = anchor[...] - mean[...]
    moved = 0.9 * momentum[...] + delta
    synced = anchor[...] - 0.7 * (delta + 0.9 * moved)
    momentum_new[...] = moved
    anchor_new[...] = synced
    weights[:, 0, :] = synced
    weights[:, 1, :] = inner[...]


def far_columns_kernel(place, far, near, out):
    out[...] = far[...]


def input_kernel(f, place, w013, w2, v013, v2, tokens, *rest):
    out, w_s, sem = (rest[0], rest[1], rest[2]) if f == 0 else (rest[1], rest[2], rest[4])
    h, c, x = place[0], place[1], place[2]
    wide, feat = w_s.shape
    rows = wide // 8
    base = h * wide if out.shape[1] > wide else 0
    copies = []
    for core, triple, last in ((c, w013, w2), (1 - c, v013, v2)):
        for step, piece, first in ((0, triple, 0), (1, triple, 1), (3, triple, 2), (2, last, 0)):
            start = pl.multiple_of((2 * lax.rem(x + step, 4) + core) * rows, 16)
            copies.append(
                pltpu.make_async_copy(
                    piece.at[pl.ds(first * rows, rows), pl.ds(f * feat, feat)],
                    w_s.at[pl.ds(start, rows)],
                    sem.at[len(copies)],
                )
            )
    for copy in copies:
        copy.start()
    for copy in copies:
        copy.wait()
    tile = 384
    dims = (((1,), (1,)), ((), ()))
    sends = []
    for j in range(wide // tile):
        cols = slice(j * tile, (j + 1) * tile)
        acc = lax.dot_general(tokens[...], w_s[cols, :], dims, preferred_element_type=F32)
        if f == 0:
            out[:, cols] = acc
            continue
        o_s, out_sem = rest[3], rest[5]
        o_s[:, cols] = (rest[0][:, cols] + acc).astype(BF16)
        sends.append(
            pltpu.make_async_copy(
                o_s.at[:, pl.ds(j * tile, tile)],
                out.at[:, pl.ds(pl.multiple_of(base + j * tile, 128), tile)],
                out_sem.at[j],
            )
        )
        sends[-1].start()
    for send in sends:
        send.wait()


def shards(activations, cotangent, weights, first_moment, second_moment, anchor, momentum):
    acts = activations[0]
    tok, width = acts.shape
    weight_here = weights[0]
    rows = weight_here.shape[0]
    feat = weight_here.shape[2]
    ylo, z, h, x, c = [lax.axis_index(a) for a in AXES]
    place = jnp.stack([h, c, x, z]).astype(jnp.int32)
    hr = rows // 2

    def whole(*dims):
        return pl.BlockSpec(dims, lambda i, place: (0,) * len(dims))

    half_rows = pl.BlockSpec((hr, feat), lambda i, place: (i, 0))
    half_both = pl.BlockSpec((hr, 2, feat), lambda i, place: (i, 0, 0))
    a_send = call(
        far_half_kernel,
        shape((tok, width // 2)),
        place,
        (acts,),
        [ANY],
        ANY,
        [pltpu.SemaphoreType.DMA],
        moved=2 * tok * width,
    )
    w0 = call(
        rounded_kernel,
        shape((rows, 2 * feat)),
        place,
        (after(weight_here, a_send),),
        [half_both],
        pl.BlockSpec((hr, 2 * feat), lambda i, place: (i, 0)),
        grid=(2,),
        moved=5 * 2**20,
        weight=WEIGHT,
    )
    w1, w3 = shift(w0, x=-1), shift(w0, x=1)
    a_far = shift(a_send, yhi=1)
    cot = after(cotangent, w0, a_send)[0]
    key, val = cot[:, 0, :], cot[:, 1, :]
    key_far = shift(key, yhi=1)

    planes = call(
        planes_kernel,
        [shape((rows, feat), F32)] * 6,
        place,
        (after(weight_here, key), first_moment[0], second_moment[0]),
        [half_both] * 3,
        [half_rows] * 6,
        grid=(2,),
        moved=14 * 2**20,
        vmem=20,
    )
    val_far = shift(after(val, planes[0]), yhi=1)

    def partial(a, c_own, c_far):
        return call(
            gradient_kernel,
            [shape((4, rows, feat))] * 2,
            place,
            (a, c_own, c_far),
            [ANY] * 3,
            [ANY] * 2,
            [
                pltpu.VMEM((2 * tok, width // 2), BF16),
                pltpu.VMEM((2 * tok, feat), BF16),
                pltpu.VMEM((width // 2, feat), BF16),
                pltpu.SemaphoreType.DMA((3,)),
                pltpu.SemaphoreType.DMA((8,)),
            ],
            flops=2 * tok * width * feat,
            moved=12 * 2**20,
            weight=WEIGHT,
            vmem=16,
        )

    def block(step):
        return pl.BlockSpec((1, rows, feat), lambda i, place: (lax.rem(place[2] + step, 4), 0, 0))

    def first_hop(mine, got):
        up, down = call(
            first_hop_kernel,
            [shape((hr, feat))] * 2,
            place,
            (mine, got),
            [block(2)] * 2,
            [whole(hr, feat)] * 2,
            moved=2**21,
        )
        return up, down

    def second_hop(mine, got, up, down, weight=0):
        return call(
            second_hop_kernel,
            [shape((rows, feat))] * 2,
            place,
            (mine, got, mine, got, up, down),
            [block(1), block(1), block(3), block(3), whole(hr, feat), whole(hr, feat)],
            [whole(rows, feat)] * 2,
            moved=2**22,
            weight=weight,
        )

    a_both = call(
        join_kernel,
        shape((2 * tok, width // 2)),
        place,
        (acts, after(a_far, planes[0])),
        [
            pl.BlockSpec((tok, width // 2), lambda i, place: (0, place[0])),
            whole(tok, width // 2),
        ],
        whole(2 * tok, width // 2),
        moved=5 * 2**20,
        weight=WEIGHT,
        vmem=16,
    )
    a_both, w1, w3, planes = lax.optimization_barrier((a_both, w1, w3, planes))
    def stack(*parts, weight=0):
        total = sum(p.shape[0] for p in parts)
        return call(
            stack_kernel,
            shape((total, 2 * feat)),
            place,
            parts,
            [whole(*p.shape) for p in parts],
            whole(total, 2 * feat),
            moved=2 * 4 * total * feat,
            weight=weight,
            vmem=20,
        )

    w2a, w2b = shift(w3[:hr], x=1), shift(w1[hr:], x=-1)
    w013 = stack(w0, w1, w3)
    v013 = shift(w013, core=1)
    mine0, other0 = partial(a_both, key, key_far)
    got0 = shift(other0, core=1)
    val_far, w2a, w2b, v013 = lax.optimization_barrier((val_far, w2a, w2b, v013))
    w2 = stack(w2a, w2b, weight=WEIGHT)
    v2 = shift(w2, core=1)
    up0, down0 = first_hop(mine0, after(got0, w2))
    up0r, down0r = shift(up0, x=1), shift(down0, x=-1)
    mine1, other1 = partial(a_both, val, after(val_far, up0))
    got1 = shift(other1, core=1)
    weights_s = pltpu.VMEM((width // 2, feat), BF16)

    def input_key(first, tokens):
        return call(
            functools.partial(input_kernel, 0),
            shape((tok, width // 2), F32),
            place,
            (first, w2, v013, v2, tokens),
            [ANY] * 4 + [whole(tok, feat)],
            whole(tok, width // 2),
            [weights_s, pltpu.SemaphoreType.DMA((8,))],
            vmem=16,
        )

    def input_val(first, tokens, key_part, columns, weight=0):
        return call(
            functools.partial(input_kernel, 1),
            shape((tok, columns)),
            place,
            (first, w2, v013, v2, tokens, key_part),
            [ANY] * 4 + [whole(tok, feat), whole(tok, width // 2)],
            ANY,
            [
                weights_s,
                pltpu.VMEM((tok, width // 2), BF16),
                pltpu.SemaphoreType.DMA((8,)),
                pltpu.SemaphoreType.DMA((6,)),
            ],
            weight=weight,
            vmem=16,
        )

    far_key = input_key(after(w013, other1), key_far)
    to_up0, to_down0 = second_hop(mine0, got0, up0r, after(down0r, far_key))
    key_parts = (shift(to_up0, x=1), shift(to_down0, x=-1))

    out_far = input_val(after(w013, to_up0), val_far, far_key, width // 2, WEIGHT)
    far = shift(out_far, yhi=1)
    up1, down1 = first_hop(mine1, after(got1, out_far))
    up1r, down1r = shift(up1, x=1), shift(down1, x=-1)
    near_key = input_key(after(w013, up1), key)
    key_parts = after(key_parts, near_key)

    half_own = pl.BlockSpec((1, hr, feat), lambda i, place: (place[2], i, 0))
    qc = feat // 4
    half_quarter = pl.BlockSpec((hr, qc), lambda i, place: (i, 0))
    sums0 = (mine0, got0, *key_parts)
    sum_specs = [half_own] * 2 + [half_rows] * 2
    own, s1, s2, s3, m_key, v_key = call(
        selected_kernel,
        [shape((rows, qc), F32)] + [shape((rows, qc))] * 3 + [shape((rows, feat), F32)] * 2,
        place,
        (*planes[:3], *sums0),
        [half_rows] * 3 + sum_specs,
        [half_quarter] * 4 + [half_rows] * 2,
        [pltpu.VMEM((hr, feat), F32)],
        grid=(2,),
        moved=10 * 2**20,
        weight=WEIGHT,
    )
    to_up1, to_down1 = second_hop(mine1, got1, up1r, after(down1r, own))
    val_parts = (shift(to_up1, x=1), shift(to_down1, x=-1))
    parts = [shift(part, z=step) for step, part in ((1, s1), (2, s2), (-1, s3))]
    total = own
    for part in parts:
        total = total + part.astype(F32)
    near = input_val(after(w013, total), val, near_key, width)
    total = lax.reduce_precision(total, 8, 7)
    total = total + after(shift(total.astype(BF16), ylo=1), near).astype(F32)
    mean = (total / 8).astype(BF16)
    means = (mean, shift(mean, z=-1), shift(mean, z=2), shift(mean, z=1))
    input_grad = call(
        far_columns_kernel,
        shape((tok, width)),
        place,
        (after(far, mean), near),
        [pl.BlockSpec((tok // 2, width // 2), lambda i, place: (i, 0)), ANY],
        pl.BlockSpec((tok // 2, width // 2), lambda i, place: (i, 1 - place[0])),
        grid=(2,),
        moved=2 * tok * width,
        alias={2: 0},
    )
    sums1 = (after(mine1, input_grad), got1, *val_parts)
    first_out, second_out, inner = call(
        moments_kernel,
        [shape((rows, 2, feat), F32)] * 2 + [shape((rows, feat), F32)],
        place,
        (m_key, v_key, *planes[3:], *sums1),
        [half_rows] * 5 + sum_specs,
        [half_both] * 2 + [half_rows],
        grid=(2,),
        moved=16 * 2**20,
    )
    weights_out, anchor_out, momentum_out = call(
        outer_kernel,
        [shape((rows, 2, feat), F32)] + [shape((rows, feat), F32)] * 2,
        place,
        (*means, anchor, momentum, inner),
        [half_quarter] * 4 + [half_rows] * 3,
        [half_both] + [half_rows] * 2,
        [pltpu.VMEM((hr, feat), F32)],
        grid=(2,),
        moved=9 * 2**20,
    )

    return (
        weights_out[None],
        first_out[None],
        second_out[None],
        anchor_out,
        momentum_out,
        input_grad[None],
    )


def solution(mesh):
    fine = Mesh(mesh.devices.reshape(SIZES), AXES)
    rep, fs = ("ylo", "z"), ("yhi", "x", "core")
    in_specs = (
        P(rep, fs, None),
        P(rep, fs, None, None),
        P(rep, fs, None, None),
        P(rep, fs, None, None),
        P(rep, fs, None, None),
        P(fs, None),
        P(fs, None),
    )
    out_specs = (
        P(rep, fs, None, None),
        P(rep, fs, None, None),
        P(rep, fs, None, None),
        P(fs, None),
        P(fs, None),
        P(rep, fs, None),
    )
    return jax.shard_map(shards, mesh=fine, in_specs=in_specs, out_specs=out_specs, check_vma=False)
```

```python
import functools

import jax
import jax.numpy as jnp
import numpy as np
from jax import lax
from jax.experimental import pallas as pl
from jax.experimental.pallas import tpu as pltpu
from jax.sharding import Mesh
from jax.sharding import PartitionSpec as P

CORRECT_FIRST = 1.0 - 0.9**8
CORRECT_SECOND = 1.0 - 0.95**8
AXES = ("ylo", "z", "yhi", "x", "core")
SIZES = (2, 4, 2, 4, 2)
BF16 = jnp.bfloat16
F32 = jnp.float32
ANY = pl.BlockSpec(memory_space=pl.ANY)
HBM = pl.BlockSpec(memory_space=pltpu.HBM)
WEIGHT = 50


def shift(value, **steps):
    pairs = []
    for source in np.ndindex(*SIZES):
        target = [(s + steps.get(a, 0)) % n for s, a, n in zip(source, AXES, SIZES)]
        pairs.append(
            (int(np.ravel_multi_index(source, SIZES)), int(np.ravel_multi_index(target, SIZES)))
        )
    return lax.ppermute(value, AXES, pairs)


def call(
    kernel, out_shape, place, inputs, in_specs, out_specs, scratch=(), grid=(1,), flops=0, moved=0, weight=0, alias=None, vmem=12
):
    return pl.pallas_call(
        kernel,
        out_shape=out_shape,
        grid_spec=pltpu.PrefetchScalarGridSpec(
            num_scalar_prefetch=1,
            grid=grid,
            in_specs=in_specs,
            out_specs=out_specs,
            scratch_shapes=list(scratch),
        ),
        compiler_params=pltpu.CompilerParams(vmem_limit_bytes=vmem * 2**20),
        input_output_aliases=alias or {},
        cost_estimate=pl.CostEstimate(flops=weight * 10**9, bytes_accessed=weight * 10**7, transcendentals=0),
    )(place, *inputs)


def after(value, *others):
    return lax.optimization_barrier((value, *others))[0]


def shape(dims, dtype=BF16):
    return jax.ShapeDtypeStruct(dims, dtype)


def far_half_kernel(place, acts, out, sem):
    n = out.shape[1]
    copy = pltpu.make_async_copy(
        acts.at[:, pl.ds(pl.multiple_of((1 - place[0]) * n, 128), n)], out, sem
    )
    copy.start()
    copy.wait()


def stack_kernel(place, *refs):
    out = refs[-1]
    n = 0
    for ref in refs[:-1]:
        out[n : n + ref.shape[0]] = ref[...]
        n += ref.shape[0]


def join_kernel(place, own, far, both):
    n = own.shape[0]
    both[:n] = own[...]
    both[n:] = far[...]


def gradient_kernel(place, a_both, c_own, c_far, mine, other, a_s, c_s, g_s, in_sem, out_sem):
    c = place[1]
    tok, wide = c_own.shape[0], a_both.shape[1]
    rows = mine.shape[1]
    copies = [
        pltpu.make_async_copy(a_both, a_s, in_sem.at[0]),
        pltpu.make_async_copy(c_own, c_s.at[pl.ds(0, tok)], in_sem.at[1]),
        pltpu.make_async_copy(c_far, c_s.at[pl.ds(tok, tok)], in_sem.at[2]),
    ]
    for copy in copies:
        copy.start()
    for copy in copies:
        copy.wait()
    tile = 256
    sends = []
    for i in range(wide // tile):
        cols = slice(i * tile, (i + 1) * tile)
        g_s[cols, :] = lax.dot_general(
            a_s[:, cols], c_s[...], (((0,), (0,)), ((), ())), preferred_element_type=F32
        ).astype(BF16)
        ready = {4: (0, 1), 8: (2, 3)}.get(i, ())
        for core, out in ((1 - c, other), (c, mine)):
            for to in ready:
                start = pl.multiple_of((2 * to + core) * rows, 16)
                sends.append(
                    pltpu.make_async_copy(
                        g_s.at[pl.ds(start, rows)], out.at[to], out_sem.at[len(sends)]
                    )
                )
                sends[-1].start()
    for send in sends:
        send.wait()


def rounded_kernel(place, w, w_low):
    n = w.shape[2]
    w_low[:, :n] = w[:, 0, :].astype(BF16)
    w_low[:, n:] = w[:, 1, :].astype(BF16)


def planes_kernel(place, w, m, v, *planes):
    for f in range(2):
        for whole, plane in zip((w, m, v), planes[3 * f : 3 * f + 3]):
            plane[...] = whole[:, f, :]


def block_sum(mine, got):
    return mine[0].astype(F32) + got[0].astype(F32)


def first_hop_kernel(place, mine, got, up, down):
    part = block_sum(mine, got).astype(BF16)
    n = up.shape[0]
    up[...] = part[:n]
    down[...] = part[n:]


def second_hop_kernel(place, mine_up, got_up, mine_down, got_down, up, down, to_up, to_down):
    n = up.shape[0]
    part = block_sum(mine_up, got_up)
    to_up[:n] = (part[:n] + up[...].astype(F32)).astype(BF16)
    to_up[n:] = part[n:].astype(BF16)
    part = block_sum(mine_down, got_down)
    to_down[:n] = part[:n].astype(BF16)
    to_down[n:] = (part[n:] + down[...].astype(F32)).astype(BF16)


def owned_sum(mine, got, *others):
    total = block_sum(mine, got)
    for other in others:
        total = total + other[...].astype(F32)
    return total


def adamw(w, m, v, g):
    m = 0.9 * m + 0.1 * g
    v = 0.95 * v + 0.05 * g * g
    step_dir = m / CORRECT_FIRST / (jnp.sqrt(v / CORRECT_SECOND) + 1e-08)
    return m, v, w - 0.01 * (step_dir + 0.1 * w)


def selected_kernel(place, w, m, v, mine, got, r1, r2, own, s1, s2, s3, m_new, v_new, sel):
    g = owned_sum(mine, got, r1, r2)
    m_new[...], v_new[...], sel[...] = adamw(w[...], m[...], v[...], g)
    n = own.shape[1]
    for step, out in ((0, own), (1, s1), (2, s2), (3, s3)):
        start = pl.multiple_of(lax.rem(place[3] + step, 4) * n, 128)
        out[...] = sel[:, pl.ds(start, n)].astype(out.dtype)


def moments_kernel(place, m_key, v_key, w, m, v, mine, got, r1, r2, first, second, inner):
    g = owned_sum(mine, got, r1, r2)
    m_new, v_new, inner[...] = adamw(w[...], m[...], v[...], g)
    first[:, 0, :] = m_key[...]
    first[:, 1, :] = m_new
    second[:, 0, :] = v_key[...]
    second[:, 1, :] = v_new


def outer_kernel(place, m0, m1, m2, m3, anchor, momentum, inner, weights, anchor_new, momentum_new, mean):
    n = m0.shape[1]
    for step, part in enumerate((m0, m1, m2, m3)):
        start = pl.multiple_of(lax.rem(place[3] + step, 4) * n, 128)
        mean[:, pl.ds(start, n)] = part[...].astype(F32)
    delta = anchor[...] - mean[...]
    moved = 0.9 * momentum[...] + delta
    synced = anchor[...] - 0.7 * (delta + 0.9 * moved)
    momentum_new[...] = moved
    anchor_new[...] = synced
    weights[:, 0, :] = synced
    weights[:, 1, :] = inner[...]


def far_columns_kernel(place, far, near, out):
    out[...] = far[...]


def input_kernel(f, place, w013, w2, v013, v2, tokens, *rest):
    out, w_s, sem = (rest[0], rest[1], rest[2]) if f == 0 else (rest[1], rest[2], rest[4])
    h, c, x = place[0], place[1], place[2]
    wide, feat = w_s.shape
    rows = wide // 8
    base = h * wide if out.shape[1] > wide else 0
    copies = []
    for core, triple, last in ((c, w013, w2), (1 - c, v013, v2)):
        for step, piece, first in ((0, triple, 0), (1, triple, 1), (3, triple, 2), (2, last, 0)):
            start = pl.multiple_of((2 * lax.rem(x + step, 4) + core) * rows, 16)
            copies.append(
                pltpu.make_async_copy(
                    piece.at[pl.ds(first * rows, rows), pl.ds(f * feat, feat)],
                    w_s.at[pl.ds(start, rows)],
                    sem.at[len(copies)],
                )
            )
    for copy in copies:
        copy.start()
    for copy in copies:
        copy.wait()
    tile = 384
    dims = (((1,), (1,)), ((), ()))
    sends = []
    for j in range(wide // tile):
        cols = slice(j * tile, (j + 1) * tile)
        acc = lax.dot_general(tokens[...], w_s[cols, :], dims, preferred_element_type=F32)
        if f == 0:
            out[:, cols] = acc
            continue
        o_s, out_sem = rest[3], rest[5]
        o_s[:, cols] = (rest[0][:, cols] + acc).astype(BF16)
        sends.append(
            pltpu.make_async_copy(
                o_s.at[:, pl.ds(j * tile, tile)],
                out.at[:, pl.ds(pl.multiple_of(base + j * tile, 128), tile)],
                out_sem.at[j],
            )
        )
        sends[-1].start()
    for send in sends:
        send.wait()


def shards(activations, cotangent, weights, first_moment, second_moment, anchor, momentum):
    acts = activations[0]
    tok, width = acts.shape
    weight_here = weights[0]
    rows = weight_here.shape[0]
    feat = weight_here.shape[2]
    ylo, z, h, x, c = [lax.axis_index(a) for a in AXES]
    place = jnp.stack([h, c, x, z]).astype(jnp.int32)
    hr = rows // 2

    def whole(*dims):
        return pl.BlockSpec(dims, lambda i, place: (0,) * len(dims))

    half_rows = pl.BlockSpec((hr, feat), lambda i, place: (i, 0))
    half_both = pl.BlockSpec((hr, 2, feat), lambda i, place: (i, 0, 0))
    a_send = call(
        far_half_kernel,
        shape((tok, width // 2)),
        place,
        (acts,),
        [ANY],
        ANY,
        [pltpu.SemaphoreType.DMA],
        moved=2 * tok * width,
    )
    w0 = call(
        rounded_kernel,
        shape((rows, 2 * feat)),
        place,
        (after(weight_here, a_send),),
        [half_both],
        pl.BlockSpec((hr, 2 * feat), lambda i, place: (i, 0)),
        grid=(2,),
        moved=5 * 2**20,
        weight=WEIGHT,
    )
    w1, w3 = shift(w0, x=-1), shift(w0, x=1)
    a_far = shift(a_send, yhi=1)
    cot = after(cotangent, w0, a_send)[0]
    key, val = cot[:, 0, :], cot[:, 1, :]
    key_far = shift(key, yhi=1)

    planes = call(
        planes_kernel,
        [shape((rows, feat), F32)] * 6,
        place,
        (after(weight_here, key), first_moment[0], second_moment[0]),
        [half_both] * 3,
        [half_rows] * 6,
        grid=(2,),
        moved=14 * 2**20,
        vmem=20,
    )
    val_far = shift(after(val, planes[0]), yhi=1)

    def partial(a, c_own, c_far):
        return call(
            gradient_kernel,
            [shape((4, rows, feat))] * 2,
            place,
            (a, c_own, c_far),
            [ANY] * 3,
            [ANY] * 2,
            [
                pltpu.VMEM((2 * tok, width // 2), BF16),
                pltpu.VMEM((2 * tok, feat), BF16),
                pltpu.VMEM((width // 2, feat), BF16),
                pltpu.SemaphoreType.DMA((3,)),
                pltpu.SemaphoreType.DMA((8,)),
            ],
            flops=2 * tok * width * feat,
            moved=12 * 2**20,
            weight=WEIGHT,
            vmem=16,
        )

    def block(step):
        return pl.BlockSpec((1, rows, feat), lambda i, place: (lax.rem(place[2] + step, 4), 0, 0))

    def first_hop(mine, got):
        up, down = call(
            first_hop_kernel,
            [shape((hr, feat))] * 2,
            place,
            (mine, got),
            [block(2)] * 2,
            [whole(hr, feat)] * 2,
            moved=2**21,
        )
        return up, down

    def second_hop(mine, got, up, down, weight=0):
        return call(
            second_hop_kernel,
            [shape((rows, feat))] * 2,
            place,
            (mine, got, mine, got, up, down),
            [block(1), block(1), block(3), block(3), whole(hr, feat), whole(hr, feat)],
            [whole(rows, feat)] * 2,
            moved=2**22,
            weight=weight,
        )

    a_both = call(
        join_kernel,
        shape((2 * tok, width // 2)),
        place,
        (acts, after(a_far, planes[0])),
        [
            pl.BlockSpec((tok, width // 2), lambda i, place: (0, place[0])),
            whole(tok, width // 2),
        ],
        whole(2 * tok, width // 2),
        moved=5 * 2**20,
        weight=WEIGHT,
        vmem=16,
    )
    a_both, w1, w3, planes = lax.optimization_barrier((a_both, w1, w3, planes))
    def stack(*parts, weight=0):
        total = sum(p.shape[0] for p in parts)
        return call(
            stack_kernel,
            shape((total, 2 * feat)),
            place,
            parts,
            [whole(*p.shape) for p in parts],
            whole(total, 2 * feat),
            moved=2 * 4 * total * feat,
            weight=weight,
            vmem=20,
        )

    w2a, w2b = shift(w3[:hr], x=1), shift(w1[hr:], x=-1)
    w013 = stack(w0, w1, w3)
    v013 = shift(w013, core=1)
    mine0, other0 = partial(a_both, key, key_far)
    got0 = shift(other0, core=1)
    val_far, w2a, w2b, v013 = lax.optimization_barrier((val_far, w2a, w2b, v013))
    w2 = stack(w2a, w2b, weight=WEIGHT)
    v2 = shift(w2, core=1)
    up0, down0 = first_hop(mine0, after(got0, w2))
    up0r, down0r = shift(up0, x=1), shift(down0, x=-1)
    mine1, other1 = partial(a_both, val, after(val_far, up0))
    got1 = shift(other1, core=1)
    weights_s = pltpu.VMEM((width // 2, feat), BF16)

    def input_key(first, tokens):
        return call(
            functools.partial(input_kernel, 0),
            shape((tok, width // 2), F32),
            place,
            (first, w2, v013, v2, tokens),
            [ANY] * 4 + [whole(tok, feat)],
            whole(tok, width // 2),
            [weights_s, pltpu.SemaphoreType.DMA((8,))],
            vmem=16,
        )

    def input_val(first, tokens, key_part, columns, weight=0):
        return call(
            functools.partial(input_kernel, 1),
            shape((tok, columns)),
            place,
            (first, w2, v013, v2, tokens, key_part),
            [ANY] * 4 + [whole(tok, feat), whole(tok, width // 2)],
            ANY,
            [
                weights_s,
                pltpu.VMEM((tok, width // 2), BF16),
                pltpu.SemaphoreType.DMA((8,)),
                pltpu.SemaphoreType.DMA((6,)),
            ],
            weight=weight,
            vmem=16,
        )

    far_key = input_key(after(w013, other1), key_far)
    to_up0, to_down0 = second_hop(mine0, got0, up0r, after(down0r, far_key))
    key_parts = (shift(to_up0, x=1), shift(to_down0, x=-1))

    out_far = input_val(after(w013, to_up0), val_far, far_key, width // 2, WEIGHT)
    far = shift(out_far, yhi=1)
    up1, down1 = first_hop(mine1, after(got1, out_far))
    up1r, down1r = shift(up1, x=1), shift(down1, x=-1)
    near_key = input_key(after(w013, up1), key)
    key_parts = after(key_parts, near_key)

    half_own = pl.BlockSpec((1, hr, feat), lambda i, place: (place[2], i, 0))
    qc = feat // 4
    half_quarter = pl.BlockSpec((hr, qc), lambda i, place: (i, 0))
    sums0 = (mine0, got0, *key_parts)
    sum_specs = [half_own] * 2 + [half_rows] * 2
    own, s1, s2, s3, m_key, v_key = call(
        selected_kernel,
        [shape((rows, qc), F32)] + [shape((rows, qc))] * 3 + [shape((rows, feat), F32)] * 2,
        place,
        (*planes[:3], *sums0),
        [half_rows] * 3 + sum_specs,
        [half_quarter] * 4 + [half_rows] * 2,
        [pltpu.VMEM((hr, feat), F32)],
        grid=(2,),
        moved=10 * 2**20,
        weight=WEIGHT,
    )
    to_up1, to_down1 = second_hop(mine1, got1, up1r, after(down1r, own))
    val_parts = (shift(to_up1, x=1), shift(to_down1, x=-1))
    parts = [shift(part, z=step) for step, part in ((1, s1), (2, s2), (-1, s3))]
    total = own
    for part in parts:
        total = total + part.astype(F32)
    near = input_val(after(w013, total), val, near_key, width)
    total = lax.reduce_precision(total, 8, 7)
    total = total + after(shift(total.astype(BF16), ylo=1), near).astype(F32)
    mean = (total / 8).astype(BF16)
    means = (mean, shift(mean, z=-1), shift(mean, z=2), shift(mean, z=1))
    input_grad = call(
        far_columns_kernel,
        shape((tok, width)),
        place,
        (after(far, mean), near),
        [pl.BlockSpec((tok // 2, width // 2), lambda i, place: (i, 0)), ANY],
        pl.BlockSpec((tok // 2, width // 2), lambda i, place: (i, 1 - place[0])),
        grid=(2,),
        moved=2 * tok * width,
        alias={2: 0},
    )
    sums1 = (after(mine1, input_grad), got1, *val_parts)
    first_out, second_out, inner = call(
        moments_kernel,
        [shape((rows, 2, feat), F32)] * 2 + [shape((rows, feat), F32)],
        place,
        (m_key, v_key, *planes[3:], *sums1),
        [half_rows] * 5 + sum_specs,
        [half_both] * 2 + [half_rows],
        grid=(2,),
        moved=16 * 2**20,
    )
    weights_out, anchor_out, momentum_out = call(
        outer_kernel,
        [shape((rows, 2, feat), F32)] + [shape((rows, feat), F32)] * 2,
        place,
        (*means, anchor, momentum, inner),
        [whole(rows, qc)] * 4 + [whole(rows, feat)] * 3,
        [whole(rows, 2, feat)] + [whole(rows, feat)] * 2,
        [pltpu.VMEM((rows, feat), F32)],
        moved=9 * 2**20,
        vmem=24,
    )

    return (
        weights_out[None],
        first_out[None],
        second_out[None],
        anchor_out,
        momentum_out,
        input_grad[None],
    )


def solution(mesh):
    fine = Mesh(mesh.devices.reshape(SIZES), AXES)
    rep, fs = ("ylo", "z"), ("yhi", "x", "core")
    in_specs = (
        P(rep, fs, None),
        P(rep, fs, None, None),
        P(rep, fs, None, None),
        P(rep, fs, None, None),
        P(rep, fs, None, None),
        P(fs, None),
        P(fs, None),
    )
    out_specs = (
        P(rep, fs, None, None),
        P(rep, fs, None, None),
        P(rep, fs, None, None),
        P(fs, None),
        P(fs, None),
        P(rep, fs, None),
    )
    return jax.shard_map(shards, mesh=fine, in_specs=in_specs, out_specs=out_specs, check_vma=False)
```
